32 devices in a mesh: row: 2 (over y), col: 16 (over z, x, core).
Axes of the slice: x: 2, y: 2, z: 4, core: 2. Of those that a mesh axis runs over, the one named last changes fastest.
Arguments:
- region: bfloat16 [32, 768, 96], P('row', 'col'), may hold values from -6 to 6
- cotangent: bfloat16 [32, 768, 96], P('row', 'col'), may hold values from -6 to 6
- norm_gains: float32 [2, 2, 96], replicated, may hold values from 0.5 to 1.5
- qkv_weight: bfloat16 [2, 96, 288], replicated, may hold values from -0.625 to 0.625
- qkv_bias: float32 [2, 288], replicated, may hold values from -3 to 3
- bias_table: float32 [2, 3, 225], replicated, may hold values from -4 to 300
- proj_weight: bfloat16 [2, 96, 96], replicated, may hold values from -0.625 to 0.625
- up_weight: bfloat16 [2, 96, 384], replicated, may hold values from -0.625 to 0.625
- up_bias: float32 [2, 384], replicated, may hold values from -3 to 3
- down_weight: bfloat16 [2, 384, 96], replicated, may hold values from -0.3125 to 0.3125
Outputs:
- output: bfloat16 [32, 768, 96], P('row', 'col')
- grad_region: float32 [32, 768, 96], P('row', 'col')
- grad_gains: float32 [2, 2, 96], replicated
- grad_qkv_weight: float32 [2, 96, 288], replicated
- grad_qkv_bias: float32 [2, 288], replicated
- grad_table: float32 [2, 3, 225], replicated
- grad_proj: float32 [2, 96, 96], replicated
- grad_up_weight: float32 [2, 96, 384], replicated
- grad_up_bias: float32 [2, 384], replicated
- grad_down_weight: float32 [2, 384, 96], replicated
The draws below stay inside these ranges and needn't reach their ends.
All inputs are finite; a program needn't handle non-finite values.
Results may differ from the reference program's by a relative error of at most 0.025.
Values may be sent and summed in bfloat16 or wider, within the bound.
A program may use at most 64 MiB of HBM per device.

```python
import jax
import jax.numpy as jnp
from jax import lax

C = 96
HEADS = 3
HID = 384
WIN = 8
TH = 16
TW = 48
TABLE = 225
ROWS = 32
COLS = 768
N_ROW = 2
N_COL = 16


def draw_bias_table(key, part):
    key = jax.random.fold_in(key, 11)
    base_key = jax.random.fold_in(key, 0)
    return jnp.clip(jax.random.normal(base_key, (2, HEADS, TABLE), jnp.float32), -4.0, 4.0)


def levels(stream_key, shape, cuts, smallest, largest):
    def one(axis_at, parts):
        heights = jax.random.uniform(jax.random.fold_in(jax.random.fold_in(stream_key, 6), axis_at), (parts,), jnp.float32, smallest / len(cuts), largest / len(cuts))
        return jnp.repeat(jnp.exp(heights), shape[axis_at] // parts).reshape((-1,) + (1,) * (len(shape) - axis_at - 1))

    level = one(*cuts[0])
    for cut in cuts[1:]:
        level = level * one(*cut)
    return level


def gaussian(stream_key, shape, deviation, bound, shards=(), kind=jnp.bfloat16):
    entries = deviation * jax.random.normal(stream_key, shape, jnp.float32)
    if shards:
        entries = entries * levels(stream_key, shape, shards, -0.22, 0.18)
    return jnp.clip(entries, -bound, bound).astype(kind)


def setup_inputs(seed: int = 0) -> dict:
    streams_of = jax.random.split(jax.random.key(seed), 11)
    region = gaussian(streams_of[0], (ROWS, COLS, C), 1.0, 6.0, ((0, 2), (1, 16)))
    cotangent = gaussian(streams_of[1], (ROWS, COLS, C), 1.0, 6.0, ((0, 2), (1, 16)))
    norm_gains = jnp.clip(1.0 + 0.1 * jax.random.normal(streams_of[2], (2, 2, C), jnp.float32), 0.5, 1.5)
    qkv_weight = gaussian(streams_of[3], (2, C, 3 * C), C ** -0.5, 0.625)
    qkv_bias = gaussian(streams_of[4], (2, 3 * C), 0.5, 3.0, (), jnp.float32)
    bias_table = draw_bias_table(jax.random.fold_in(streams_of[10], 71), 0)
    proj_weight = gaussian(streams_of[6], (2, C, C), C ** -0.5, 0.625)
    up_weight = gaussian(streams_of[7], (2, C, HID), C ** -0.5, 0.625)
    up_bias = gaussian(streams_of[8], (2, HID), 0.5, 3.0, (), jnp.float32)
    down_weight = gaussian(streams_of[9], (2, HID, C), HID ** -0.5, 0.3125)
    return dict(region=region, cotangent=cotangent, norm_gains=norm_gains, qkv_weight=qkv_weight, qkv_bias=qkv_bias, bias_table=bias_table, proj_weight=proj_weight, up_weight=up_weight, up_bias=up_bias, down_weight=down_weight)


HIGHEST = lax.Precision.HIGHEST

def layer_norm(values, gain):
    average = lax.optimization_barrier(jnp.mean(values, -1, keepdims=True))
    centred = values - average
    variance = lax.optimization_barrier(jnp.mean(centred * centred, -1, keepdims=True))
    return centred * lax.rsqrt(variance + 1e-05) * gain

def position_bias(table):
    positions = jnp.arange(WIN * WIN, dtype=jnp.int32)
    pos_row = positions // WIN
    pos_col = positions % WIN
    table_side = 2 * WIN - 1
    table_index = (pos_row[:, None] - pos_row[None, :] + WIN - 1) * table_side + (pos_col[:, None] - pos_col[None, :] + WIN - 1)
    onehot = (table_index[:, :, None] == jnp.arange(table_side * table_side, dtype=jnp.int32)[None, None, :]).astype(jnp.float32)
    return jnp.einsum('qkt,ht->hqk', onehot, table, precision=HIGHEST)

def windowize(field):
    height, width, depth = field.shape
    blocks = field.reshape(height // WIN, WIN, width // WIN, WIN, depth)
    return blocks.transpose(0, 2, 1, 3, 4).reshape(-1, WIN * WIN, depth)

def unwindowize(windows, height, width):
    depth = windows.shape[-1]
    blocks = windows.reshape(height // WIN, width // WIN, WIN, WIN, depth)
    return blocks.transpose(0, 2, 1, 3, 4).reshape(height, width, depth)

def attend(windows, usable, layer):
    gain_pair, qkv_weight, qkv_bias, table, proj_weight = layer[:5]
    win_count, win_tokens, channels = windows.shape
    head_count = table.shape[0]
    head_size = channels // head_count
    normed = layer_norm(windows, gain_pair[0]).astype(jnp.bfloat16).reshape(win_count * win_tokens, channels)
    triple = (jnp.dot(normed, qkv_weight, preferred_element_type=jnp.float32) + qkv_bias).astype(jnp.bfloat16)
    triple = triple.reshape(win_count, win_tokens, 3, head_count, head_size)
    queries = triple[:, :, 0].astype(jnp.float32)
    key_part = triple[:, :, 1].astype(jnp.float32)
    value_part = triple[:, :, 2].astype(jnp.float32)
    scores = jnp.einsum('wqhd,wkhd->whqk', queries, key_part) * head_size ** (-0.5) + position_bias(table)[None]
    if usable is not None:
        scores = jnp.where(usable[:, None, None, :], scores, -1e+30)
    highest = lax.stop_gradient(lax.optimization_barrier(jnp.max(scores, -1, keepdims=True)))
    exponent = jnp.exp(scores - highest)
    softmax_w = (exponent / lax.optimization_barrier(jnp.sum(exponent, -1, keepdims=True))).astype(jnp.bfloat16)
    mixture = jnp.einsum('whqk,wkhd->wqhd', softmax_w.astype(jnp.float32), value_part).astype(jnp.bfloat16)
    mixture = mixture.reshape(win_count * win_tokens, channels)
    projected = jnp.dot(mixture, proj_weight, preferred_element_type=jnp.float32)
    return windows + projected.reshape(win_count, win_tokens, channels)

def feed(field, layer):
    gain_pair = layer[0]
    up_weight, up_bias, down_weight = layer[5:]
    channels = field.shape[-1]
    flat_rows = field.reshape(-1, channels)
    normed = layer_norm(flat_rows, gain_pair[1]).astype(jnp.bfloat16)
    hidden = jax.nn.gelu(jnp.dot(normed, up_weight, preferred_element_type=jnp.float32) + up_bias).astype(jnp.bfloat16)
    return (flat_rows + jnp.dot(hidden, down_weight, preferred_element_type=jnp.float32)).reshape(field.shape)

def regular(field, layer):
    height, width, _ = field.shape
    return feed(unwindowize(attend(windowize(field), None, layer), height, width), layer)

def shifted(padded, row_start, col_start, total_rows, total_cols, layer):
    half_win = WIN // 2
    height = padded.shape[0] - WIN
    width = padded.shape[1] - WIN
    row_ids = row_start + jnp.arange(height + WIN, dtype=jnp.int32)
    col_ids = col_start + jnp.arange(width + WIN, dtype=jnp.int32)
    inside = ((row_ids >= 0) & (row_ids < total_rows))[:, None] & ((col_ids >= 0) & (col_ids < total_cols))[None, :]
    usable = windowize(inside[:, :, None]).reshape(-1, WIN * WIN)
    mixed_field = unwindowize(attend(windowize(padded), usable, layer), height + WIN, width + WIN)
    return feed(mixed_field[half_win:half_win + height, half_win:half_win + width], layer)

def to_tiles(field):
    depth = field.shape[-1]
    return field.reshape(N_ROW, TH, N_COL, TW, depth).transpose(0, 2, 1, 3, 4).reshape(N_ROW * N_COL, TH, TW, depth)

def from_tiles(tiles):
    depth = tiles.shape[-1]
    return tiles.reshape(N_ROW, N_COL, TH, TW, depth).transpose(0, 2, 1, 3, 4).reshape(ROWS, COLS, depth)

def reference(region, cotangent, norm_gains, qkv_weight, qkv_bias, bias_table, proj_weight, up_weight, up_bias, down_weight):
    stacked = (norm_gains, qkv_weight, qkv_bias, bias_table, proj_weight, up_weight, up_bias, down_weight)
    lower_layer = tuple((entry[0] for entry in stacked))
    upper_layer = tuple((entry[1] for entry in stacked))
    half_win = WIN // 2
    region_tiles = to_tiles(region)
    cot_tiles = to_tiles(cotangent)
    lower_tiles = lax.map(lambda tile_in: regular(tile_in.astype(jnp.float32), lower_layer).astype(jnp.bfloat16), region_tiles)
    padded = jnp.pad(from_tiles(lower_tiles), ((half_win, half_win), (half_win, half_win), (0, 0)))
    zero_sums = tuple((jnp.zeros(entry.shape, jnp.float32) for entry in upper_layer))

    def upper_step(state_pair, number):
        grad_field, totals = state_pair
        tile_row = number // N_COL
        tile_col = number % N_COL
        starts = ((tile_row * TH).astype(jnp.int32), (tile_col * TW).astype(jnp.int32), jnp.zeros((), jnp.int32))
        patch = lax.dynamic_slice(padded, starts, (TH + WIN, TW + WIN, C)).astype(jnp.float32)

        def upper_block(field, layer):
            return shifted(field, tile_row * TH - half_win, tile_col * TW - half_win, ROWS, COLS, layer)
        result, pull_upper = jax.vjp(upper_block, patch, upper_layer)
        grad_patch, grad_layer = pull_upper(cot_tiles[number].astype(jnp.float32))
        current = lax.dynamic_slice(grad_field, starts, grad_patch.shape)
        grad_field = lax.dynamic_update_slice(grad_field, current + grad_patch, starts)
        totals = tuple((total + part.astype(jnp.float32) for total, part in zip(totals, grad_layer)))
        return ((grad_field, totals), result.astype(jnp.bfloat16))
    start_field = jnp.zeros((ROWS + WIN, COLS + WIN, C), jnp.float32)
    (grad_field, upper_totals), upper_tiles = lax.scan(upper_step, (start_field, zero_sums), jnp.arange(N_ROW * N_COL, dtype=jnp.int32))
    grad_lower = grad_field[half_win:half_win + ROWS, half_win:half_win + COLS]

    def lower_step(totals, pair):
        tile_in, tile_grad = pair
        _, pull_lower = jax.vjp(regular, tile_in.astype(jnp.float32), lower_layer)
        grad_tile, grad_layer = pull_lower(tile_grad)
        totals = tuple((total + part.astype(jnp.float32) for total, part in zip(totals, grad_layer)))
        return (totals, grad_tile)
    lower_totals, grad_tiles = lax.scan(lower_step, zero_sums, (region_tiles, to_tiles(grad_lower)))
    grads = [jnp.stack([low_part, up_part]) for low_part, up_part in zip(lower_totals, upper_totals)]
    return (from_tiles(upper_tiles), from_tiles(grad_tiles), grads[0], grads[1], grads[2], grads[3], grads[4], grads[5], grads[6], grads[7])
```

```python
import functools

import jax
import jax.numpy as jnp
from jax import lax
from jax.experimental import pallas as pl
from jax.experimental.pallas import tpu as pltpu
from jax.sharding import PartitionSpec as P

WIN = 8
HALF = 4
TOK = 64
BF = jnp.bfloat16
F32 = jnp.float32
MESH = pl.DeviceIdType.MESH

U_QKV = 0
U_PROJ = 18
U_UP = 24
U_DOWN = 42
U_SMALL = 60
U_BLOCK = 62


def dot_nn(a, b):
    return lax.dot_general(a, b, (((1,), (0,)), ((), ())), preferred_element_type=F32)


def dot_nt(a, b):
    return lax.dot_general(a, b, (((1,), (1,)), ((), ())), preferred_element_type=F32)


def dot_tn(a, b):
    return lax.dot_general(a, b, (((0,), (0,)), ((), ())), preferred_element_type=F32)


def norm(x):
    average = jnp.mean(x, -1, keepdims=True)
    centred = x - average
    rstd = lax.rsqrt(jnp.mean(centred * centred, -1, keepdims=True) + 1e-05)
    return centred * rstd, rstd


def norm_back(dy, gain, xhat, rstd):
    dx = dy * gain
    return rstd * (
        dx - jnp.mean(dx, -1, keepdims=True) - xhat * jnp.mean(dx * xhat, -1, keepdims=True)
    )


def seg_first(shape):
    return lax.broadcasted_iota(jnp.int32, shape, 1) < TOK


def seg_reduce(fn, fill, s):
    lo, hi = s[:, :128], s[:, 128:]
    first = seg_first(lo.shape)
    r0 = fn(jnp.where(first, lo, fill), -1, keepdims=True)
    r1 = fn(jnp.where(first, fill, lo), -1, keepdims=True)
    r2 = fn(hi, -1, keepdims=True)
    return r0, r1, r2


def seg_spread(parts, like):
    r0, r1, r2 = parts
    lo = jnp.where(seg_first((like.shape[0], 128)), r0, r1)
    hi = jnp.broadcast_to(r2, (like.shape[0], 64))
    return jnp.concatenate([lo, hi], 1)


def softmax(s):
    e = jnp.exp(s - seg_spread(seg_reduce(jnp.max, -jnp.inf, s), s))
    sums = seg_reduce(jnp.sum, 0.0, e)
    return e * seg_spread(tuple(1.0 / t for t in sums), s)


def head_masks(channels):
    lane = lax.broadcasted_iota(jnp.int32, (1, channels), 1)
    size = channels // 3
    return [((lane >= h * size) & (lane < (h + 1) * size)) for h in range(3)]


def stack_heads(x, masks):
    zero = jnp.zeros_like(x)
    return jnp.concatenate([jnp.where(m, x, zero) for m in masks], 0)


def fold_heads(x, masks):
    out = jnp.where(masks[0], x[:TOK], 0.0)
    for h in (1, 2):
        out = out + jnp.where(masks[h], x[h * TOK : (h + 1) * TOK], 0.0)
    return out


def factors(n_row, n_col):
    phases = [[("col", 1, 2)], [("col", 2, 2), ("row", 1, n_row)], [("col", 4, n_col // 4)]]
    phases = [[f for f in p if f[2] > 1] for p in phases]
    return [p for p in phases if p]


def kernel(
    n_row,
    n_col,
    units,
    region,
    cot,
    gains,
    wqkv,
    bqkv,
    xtab,
    wproj,
    wup,
    bup,
    wdown,
    out,
    grad_region,
    o_qkv,
    o_proj,
    o_up,
    o_down,
    o_small,
    ws,
    bias,
    f0,
    h0,
    f1,
    h1,
    dh1,
    g1,
    a_qkv,
    a_proj,
    a_up,
    a_down,
    a_vec,
    a_bup,
    a_bias,
    hs_row,
    hr_row,
    hs_col,
    hr_col,
    halo_send,
    halo_recv,
    pack,
    *rest,
):
    rows, cols, channels = region.shape
    prow, pcol = rows + WIN, cols + WIN
    scale = (channels // 3) ** (-0.5)
    phases = factors(n_row, n_col)
    n_ph = len(phases)
    rs_recv = rest[:n_ph]
    rs_acc = rest[n_ph : 2 * n_ph]
    ag_buf = rest[2 * n_ph : 3 * n_ph]
    red_send, red_recv = rest[3 * n_ph :]
    index = {"row": lax.axis_index("row"), "col": lax.axis_index("col")}
    count = {"row": n_row, "col": n_col}

    def device(changes):
        where = dict(index)
        where.update(changes)
        return (where["row"], where["col"])

    def side(axis, step):
        n = count[axis]
        return device({axis: lax.rem(index[axis] + (step + n), n)})

    def members(phase):
        size = 1
        me = 0
        for _, stride, n in phase:
            size *= n
        partners = []
        digits = []
        for axis, stride, n in phase:
            digit = lax.rem(lax.div(index[axis], stride), n)
            digits.append(digit)
            me = me * n + digit
        for d in range(1, size):
            rest_d, ds = d, []
            for _, _, n in reversed(phase):
                ds.append(rest_d % n)
                rest_d //= n
            ds = ds[::-1]
            neg = 0
            member = 0
            changes = {}
            for (axis, stride, n), digit, step in zip(phase, digits, ds):
                neg = neg * n + (-step) % n
                other = lax.rem(digit + step, n)
                member = member * n + other
                changes[axis] = changes.get(axis, index[axis]) + (other - digit) * stride
            partners.append((d, neg, member, device(changes)))
        return size, me, partners

    groups = [members(p) for p in phases]

    barrier = pltpu.get_barrier_semaphore()
    greet = [side("col", -1), side("col", 1), side("row", -1), side("row", 1)]
    for _, _, partners in groups:
        greet += [p[3] for p in partners]
    for dev in greet:
        pl.semaphore_signal(barrier, inc=1, device_id=dev, device_id_type=MESH)

    for ref in (a_qkv, a_proj, a_up, a_down, a_vec, a_bup, a_bias, dh1, f1, pack):
        ref[...] = jnp.zeros(ref.shape, ref.dtype)
    for b in range(2):
        whole = wqkv[b].astype(F32)
        for t in range(3):
            ws[b, t] = whole[:, t * channels : (t + 1) * channels].astype(BF)
        for r in range(WIN):
            at = (WIN - 1 - r) * WIN
            bias[b, r * WIN : (r + 1) * WIN, :] = jnp.concatenate(
                [xtab[b, h][:, at : at + TOK] for h in range(3)], 1
            )
    f0[...] = region[...].astype(F32)
    masks = head_masks(channels)

    def qkv_of(u, b):
        xhat, rstd = norm(u)
        a = (xhat * gains[b, 0:1, :]).astype(BF)
        line = bqkv[b : b + 1, :]
        parts = [
            (dot_nn(a, ws[b, t]) + line[:, t * channels : (t + 1) * channels]).astype(BF)
            for t in range(3)
        ]
        return xhat, rstd, a, parts

    def window(q, k, v, b, usable):
        kbd, vbd = stack_heads(k, masks), stack_heads(v, masks)
        s = dot_nt(q, kbd) * scale + bias[b]
        if usable is not None:
            s = jnp.where(usable, s, -1e30)
        return kbd, vbd, softmax(s)

    def split(x, w):
        return x[w * TOK : (w + 1) * TOK]

    def attn_forward(u, b, usable):
        _, _, _, (q, k, v) = qkv_of(u, b)
        mixed = []
        for w in range(u.shape[0] // TOK):
            _, vbd, p = window(split(q, w), split(k, w), split(v, w), b, usable[w])
            mixed.append(dot_nn(p.astype(BF), vbd))
        mixed = jnp.concatenate(mixed, 0).astype(BF)
        return u + dot_nn(mixed, wproj[b])

    def attn_backward(u, dh, b, usable):
        xhat, rstd, a, (q, k, v) = qkv_of(u, b)
        dhb = dh.astype(BF)
        dmix = dot_nt(dhb, wproj[b]).astype(BF)
        mixed, dqs, dks, dvs = [], [], [], []
        dbias = None
        for w in range(u.shape[0] // TOK):
            qw, do = split(q, w), split(dmix, w)
            kbd, vbd, p = window(qw, split(k, w), split(v, w), b, usable[w])
            pb = p.astype(BF)
            mixed.append(dot_nn(pb, vbd))
            dp = dot_nt(do, vbd)
            ds = p * (dp - seg_spread(seg_reduce(jnp.sum, 0.0, dp * p), p))
            dbias = ds if dbias is None else dbias + ds
            dsb = (ds * scale).astype(BF)
            dqs.append(dot_nn(dsb, kbd))
            dks.append(fold_heads(dot_tn(dsb, qw), masks))
            dvs.append(fold_heads(dot_tn(pb, do), masks))
        mixed = jnp.concatenate(mixed, 0).astype(BF)
        a_proj[b] += dot_tn(mixed, dhb)
        a_bias[b] += dbias
        da = None
        for t, parts in enumerate((dqs, dks, dvs)):
            grad = jnp.concatenate(parts, 0)
            a_vec[b, t : t + 1, :] += jnp.sum(grad, 0, keepdims=True)
            grad = grad.astype(BF)
            a_qkv[b, t] += dot_tn(a, grad)
            term = dot_nt(grad, ws[b, t])
            da = term if da is None else da + term
        a_vec[b, 3:4, :] += jnp.sum(da * xhat, 0, keepdims=True)
        return dh + norm_back(da, gains[b, 0:1, :], xhat, rstd)

    def gelu(z):
        t = jnp.tanh(0.7978845608028654 * z * (1.0 + 0.044715 * z * z))
        return t, 0.5 * z * (1.0 + t)

    def feed_forward(h, b):
        xhat, _ = norm(h)
        f = (xhat * gains[b, 1:2, :]).astype(BF)
        _, m = gelu(dot_nn(f, wup[b]) + bup[b : b + 1, :])
        return h + dot_nn(m.astype(BF), wdown[b])

    def feed_backward(h, g, b, want_out):
        xhat, rstd = norm(h)
        f = (xhat * gains[b, 1:2, :]).astype(BF)
        z = dot_nn(f, wup[b]) + bup[b : b + 1, :]
        t, m = gelu(z)
        m = m.astype(BF)
        result = h + dot_nn(m, wdown[b]) if want_out else None
        gb = g.astype(BF)
        dm = dot_nt(gb, wdown[b])
        slope = 0.5 * (1.0 + t) + 0.5 * z * (1.0 - t * t) * (
            0.7978845608028654 * (1.0 + 0.134145 * z * z)
        )
        dz = dm * slope
        a_bup[b : b + 1, :] += jnp.sum(dz, 0, keepdims=True)
        dz = dz.astype(BF)
        a_down[b] += dot_tn(gb, m)
        a_up[b] += dot_tn(f, dz)
        df = dot_nt(dz, wup[b])
        a_vec[b, 4:5, :] += jnp.sum(df * xhat, 0, keepdims=True)
        return result, g + norm_back(df, gains[b, 1:2, :], xhat, rstd)

    def spots0(j):
        return [(i * WIN, pl.multiple_of((j * 2 + c) * WIN, WIN)) for i in range(rows // WIN) for c in range(2)]

    def spots1(j):
        return [(i * WIN, pl.multiple_of(j * WIN, WIN)) for i in range(prow // WIN)]

    def gather(ref, spots):
        return jnp.concatenate(
            [ref[r : r + WIN, pl.ds(c, WIN), :].reshape(TOK, channels) for r, c in spots], 0
        )

    def scatter(ref, spots, x):
        for w, (r, c) in enumerate(spots):
            ref[r : r + WIN, pl.ds(c, WIN), :] = split(x, w).reshape(WIN, WIN, channels)

    lane = lax.broadcasted_iota(jnp.int32, (1, 3 * TOK), 1)
    key_row = lax.div(lax.rem(lane, TOK), WIN)
    key_col = lax.rem(lane, WIN)

    def usable1(spots):
        found = []
        for r, c in spots:
            row = key_row + (index["row"] * rows - HALF + r)
            col = key_col + (index["col"] * cols - HALF + c)
            found.append(
                (row >= 0) & (row < n_row * rows) & (col >= 0) & (col < n_col * cols)
            )
        return found

    none = [None] * 4
    n0 = cols // (2 * WIN)
    n1 = pcol // WIN
    strip = 4
    flat = strip * cols

    @pl.loop(0, n0)
    def _(j):
        spots = spots0(j)
        scatter(h0, spots, attn_forward(gather(f0, spots), 0, none))

    @pl.loop(0, rows // strip)
    def _(j):
        h = h0[pl.ds(j * strip, strip)].reshape(flat, channels)
        low = feed_forward(h, 0).astype(BF).astype(F32)
        f1[pl.ds(HALF + j * strip, strip), HALF : HALF + cols, :] = low.reshape(
            strip, cols, channels
        )

    def exchange(slot, axis, sends, recvs):
        copies = []
        for way, (step, there) in enumerate(((-1, 1), (1, 0))):
            copy = pltpu.make_async_remote_copy(
                src_ref=sends.at[slot // 2, way],
                dst_ref=recvs.at[slot // 2, there],
                send_sem=halo_send.at[2 * slot + way],
                recv_sem=halo_recv.at[2 * slot + there],
                device_id=side(axis, step),
                device_id_type=MESH,
            )
            copy.start()
            copies.append(copy)
        for copy in copies:
            copy.wait()

    pl.semaphore_wait(barrier, len(greet))

    def put_rows(at, field, first, second):
        hs_row[at, 0] = field[first : first + HALF].reshape(HALF * pcol, channels).astype(BF)
        hs_row[at, 1] = field[second : second + HALF].reshape(HALF * pcol, channels).astype(BF)

    def put_cols(at, field):
        hs_col[at, 0] = field[:, 0:WIN, :].reshape(prow * WIN, channels).astype(BF)
        hs_col[at, 1] = field[:, pcol - WIN : pcol, :].reshape(prow * WIN, channels).astype(BF)

    def got_row(at, way):
        return hr_row[at, way].astype(F32).reshape(HALF, pcol, channels)

    def got_col(at, way):
        return hr_col[at, way].astype(F32).reshape(prow, WIN, channels)

    put_rows(0, f1, HALF, rows)
    exchange(0, "row", hs_row, hr_row)
    f1[0:HALF] = got_row(0, 0)
    f1[prow - HALF : prow] = got_row(0, 1)
    put_cols(0, f1)
    exchange(1, "col", hs_col, hr_col)
    upper_half = lax.broadcasted_iota(jnp.int32, (prow, WIN, channels), 1) >= HALF
    f1[:, 0:WIN, :] = jnp.where(upper_half, f1[:, 0:WIN, :], got_col(0, 0))
    f1[:, pcol - WIN : pcol, :] = jnp.where(
        upper_half, got_col(0, 1), f1[:, pcol - WIN : pcol, :]
    )

    @pl.loop(0, n1)
    def _(j):
        spots = spots1(j)
        scatter(h1, spots, attn_forward(gather(f1, spots), 1, usable1(spots)))

    @pl.loop(0, rows // strip)
    def _(j):
        inner = pl.ds(HALF + j * strip, strip)
        h = h1[inner, HALF : HALF + cols, :].reshape(flat, channels)
        g = cot[pl.ds(j * strip, strip)].astype(F32).reshape(flat, channels)
        result, dh = feed_backward(h, g, 1, True)
        out[pl.ds(j * strip, strip)] = result.reshape(strip, cols, channels).astype(BF)
        dh1[inner, HALF : HALF + cols, :] = dh.reshape(strip, cols, channels)

    @pl.loop(0, n1)
    def _(j):
        spots = spots1(j)
        du = attn_backward(gather(f1, spots), gather(dh1, spots), 1, usable1(spots))
        scatter(g1, spots, du)

    put_cols(1, g1)
    exchange(3, "col", hs_col, hr_col)
    g1[:, 0:WIN, :] += got_col(1, 0)
    g1[:, pcol - WIN : pcol, :] += got_col(1, 1)
    put_rows(1, g1, 0, prow - HALF)
    exchange(2, "row", hs_row, hr_row)
    g1[HALF : 2 * HALF] += got_row(1, 0)
    g1[rows : rows + HALF] += got_row(1, 1)

    @pl.loop(0, rows // strip)
    def _(j):
        here = pl.ds(j * strip, strip)
        h = h0[here].reshape(flat, channels)
        g = g1[pl.ds(HALF + j * strip, strip), HALF : HALF + cols, :].reshape(flat, channels)
        _, dh = feed_backward(h, g, 0, False)
        h0[here] = dh.reshape(strip, cols, channels)

    @pl.loop(0, n0)
    def _(j):
        spots = spots0(j)
        scatter(grad_region, spots, attn_backward(gather(f0, spots), gather(h0, spots), 0, none))

    def stow(unit, x, width):
        n = x.shape[0] // 16
        for t in range((width + 127) // 128):
            part = x[:, t * 128 : min(width, (t + 1) * 128)]
            wide = part.shape[1]
            pack[unit + t * n : unit + (t + 1) * n, :, 0:wide] = part.reshape(n, 16, wide).astype(BF)

    hidden = wup.shape[2]
    for b in range(2):
        base = b * U_BLOCK
        for t in range(3):
            stow(base + U_QKV + 6 * t, a_qkv[b, t], channels)
        stow(base + U_PROJ, a_proj[b], channels)
        stow(base + U_UP, a_up[b], hidden)
        stow(base + U_DOWN, a_down[b], hidden)
        heads = []
        for h in range(3):
            total = None
            for r in range(WIN):
                at = (WIN - 1 - r) * WIN
                part = a_bias[b, r * WIN : (r + 1) * WIN, h * TOK : (h + 1) * TOK]
                pieces = [part, jnp.zeros((WIN, 128 - at - TOK), F32)]
                if at:
                    pieces = [jnp.zeros((WIN, at), F32)] + pieces
                part = jnp.concatenate(pieces, 1)
                total = part if total is None else total + part
            heads.append(total)
        vec = jnp.concatenate([a_vec[b], jnp.zeros((WIN, 128 - channels), F32)], 1)
        sub = lax.broadcasted_iota(jnp.int32, (WIN, 128), 0)
        for t in range(3):
            vec = jnp.where(sub == 5 + t, a_bup[b : b + 1, t * 128 : (t + 1) * 128], vec)
        small = jnp.concatenate([vec] + heads, 0)
        stow(base + U_SMALL, small, 128)

    source = pack
    size_now = units
    at_sem = 0
    for ph, (size, me, partners) in enumerate(groups):
        part = size_now // size
        copies = []
        for d, neg, member, dev in partners:
            copy = pltpu.make_async_remote_copy(
                src_ref=source.at[pl.ds(member * part, part)],
                dst_ref=rs_recv[ph].at[neg - 1],
                send_sem=red_send.at[at_sem + d - 1],
                recv_sem=red_recv.at[at_sem + neg - 1],
                device_id=dev,
                device_id_type=MESH,
            )
            copy.start()
            copies.append(copy)
        total = source[pl.ds(me * part, part)].astype(F32)
        for copy in copies:
            copy.wait()
        for d in range(size - 1):
            total = total + rs_recv[ph][d].astype(F32)
        rs_acc[ph][...] = total.astype(BF)
        source = rs_acc[ph]
        size_now = part
        at_sem += size - 1
    for ph in reversed(range(n_ph)):
        size, me, partners = groups[ph]
        part = size_now
        copies = []
        for d, neg, member, dev in partners:
            copy = pltpu.make_async_remote_copy(
                src_ref=source,
                dst_ref=ag_buf[ph].at[pl.ds(me * part, part)],
                send_sem=red_send.at[at_sem + d - 1],
                recv_sem=red_recv.at[at_sem + neg - 1],
                device_id=dev,
                device_id_type=MESH,
            )
            copy.start()
            copies.append(copy)
        ag_buf[ph][pl.ds(me * part, part)] = source[...]
        for copy in copies:
            copy.wait()
        source = ag_buf[ph]
        size_now = part * size
        at_sem += size - 1

    def fetch(unit, n, width=128):
        return source[unit : unit + n].astype(F32).reshape(n * 16, 128)[:, :width]

    for b in range(2):
        base = b * U_BLOCK
        for t in range(3):
            o_qkv[b, t] = fetch(base + U_QKV + 6 * t, 6, channels)
            o_up[b, :, t * 128 : (t + 1) * 128] = fetch(base + U_UP + 6 * t, 6)
            o_down[b, :, t * 128 : (t + 1) * 128] = fetch(base + U_DOWN + 6 * t, 6)
        o_proj[b] = fetch(base + U_PROJ, 6, channels)
        o_small[b] = fetch(base + U_SMALL, 2)


def expand_table(table):
    side = 2 * WIN - 1
    grid = table.reshape(2, -1, side, side)[:, :, ::-1, ::-1]
    x = jnp.stack([grid[..., WIN - 1 - c : side - c] for c in range(WIN)], 2)
    return x.reshape(2, grid.shape[1], WIN, side * WIN)


def fold_table(dx):
    side = 2 * WIN - 1
    x = dx.reshape(2, -1, WIN, side, WIN)
    total = 0.0
    for c in range(WIN):
        total = total + jnp.pad(
            x[:, :, c], ((0, 0), (0, 0), (0, 0), (WIN - 1 - c, c))
        )
    return total[:, :, ::-1, ::-1].reshape(2, -1, side * side)


def body(n_row, n_col, region, cotangent, gains, wqkv, bqkv, table, wproj, wup, bup, wdown):
    rows, cols, channels = region.shape
    hidden = wup.shape[2]
    prow, pcol = rows + WIN, cols + WIN
    devices = n_row * n_col
    units = -(-2 * U_BLOCK // devices) * devices
    phases = factors(n_row, n_col)
    sizes = []
    for phase in phases:
        size = 1
        for f in phase:
            size *= f[2]
        sizes.append(size)
    recv, acc, gath = [], [], []
    now = units
    for size in sizes:
        gath.append(pltpu.VMEM((now, 16, 128), BF))
        now //= size
        recv.append(pltpu.VMEM((size - 1, now, 16, 128), BF))
        acc.append(pltpu.VMEM((now, 16, 128), BF))
    steps = 2 * sum(s - 1 for s in sizes)
    vmem = pl.BlockSpec(memory_space=pltpu.VMEM)
    shapes = [
        jax.ShapeDtypeStruct((rows, cols, channels), BF),
        jax.ShapeDtypeStruct((rows, cols, channels), F32),
        jax.ShapeDtypeStruct((2, 3, channels, channels), F32),
        jax.ShapeDtypeStruct((2, channels, channels), F32),
        jax.ShapeDtypeStruct((2, channels, hidden), F32),
        jax.ShapeDtypeStruct((2, channels, hidden), F32),
        jax.ShapeDtypeStruct((2, 32, 128), F32),
    ]
    field0 = pltpu.VMEM((rows, cols, channels), F32)
    field1 = pltpu.VMEM((prow, pcol, channels), F32)
    results = pl.pallas_call(
        functools.partial(kernel, n_row, n_col, units),
        out_shape=shapes,
        in_specs=[vmem] * 10,
        out_specs=[vmem] * len(shapes),
        scratch_shapes=[
            pltpu.VMEM((2, 3, channels, channels), BF),
            pltpu.VMEM((2, TOK, 3 * TOK), F32),
            field0,
            field0,
            field1,
            field1,
            field1,
            field1,
            pltpu.VMEM((2, 3, channels, channels), F32),
            pltpu.VMEM((2, channels, channels), F32),
            pltpu.VMEM((2, channels, hidden), F32),
            pltpu.VMEM((2, channels, hidden), F32),
            pltpu.VMEM((2, 8, channels), F32),
            pltpu.VMEM((2, hidden), F32),
            pltpu.VMEM((2, TOK, 3 * TOK), F32),
            pltpu.VMEM((2, 2, HALF * pcol, channels), BF),
            pltpu.VMEM((2, 2, HALF * pcol, channels), BF),
            pltpu.VMEM((2, 2, prow * WIN, channels), BF),
            pltpu.VMEM((2, 2, prow * WIN, channels), BF),
            pltpu.SemaphoreType.DMA((8,)),
            pltpu.SemaphoreType.DMA((8,)),
            pltpu.VMEM((units, 16, 128), BF),
            *recv,
            *acc,
            *gath,
            pltpu.SemaphoreType.DMA((steps,)),
            pltpu.SemaphoreType.DMA((steps,)),
        ],
        compiler_params=pltpu.CompilerParams(
            collective_id=0, has_side_effects=True, vmem_limit_bytes=48 * 1024 * 1024
        ),
        name="swin_pair",
    )(region, cotangent, gains, wqkv, bqkv, expand_table(table), wproj, wup, bup, wdown)
    out, grad_region, dqkv, dproj, dup, down_t, small = results
    vec = small[:, 0:5, :channels]
    return (
        out,
        grad_region,
        vec[:, 3:5],
        dqkv.transpose(0, 2, 1, 3).reshape(2, channels, 3 * channels),
        vec[:, 0:3].reshape(2, 3 * channels),
        fold_table(small[:, 8:32, : (2 * WIN - 1) * WIN].reshape(2, 3, WIN, -1)),
        dproj,
        dup,
        small[:, 5:8].reshape(2, hidden),
        down_t.transpose(0, 2, 1),
    )


def solution(mesh):
    tile = P("row", "col", None)
    return jax.shard_map(
        functools.partial(body, mesh.shape["row"], mesh.shape["col"]),
        mesh=mesh,
        in_specs=(tile, tile) + (P(),) * 8,
        out_specs=(tile, tile) + (P(),) * 8,
        check_vma=False,
    )
```

```python
import functools

import jax
import jax.numpy as jnp
from jax import lax
from jax.experimental import pallas as pl
from jax.experimental.pallas import tpu as pltpu
from jax.sharding import PartitionSpec as P

WIN = 8
HALF = 4
TOK = 64
BF = jnp.bfloat16
F32 = jnp.float32
MESH = pl.DeviceIdType.MESH
GROUP = 6

U_QKV = 0
U_PROJ = 18
U_UP = 24
U_DOWN = 42
U_SMALL = 60
U_BLOCK = 62


def dot_nn(a, b):
    return lax.dot_general(a, b, (((1,), (0,)), ((), ())), preferred_element_type=F32)


def dot_nt(a, b):
    return lax.dot_general(a, b, (((1,), (1,)), ((), ())), preferred_element_type=F32)


def dot_tn(a, b):
    return lax.dot_general(a, b, (((0,), (0,)), ((), ())), preferred_element_type=F32)


def norm(x):
    average = jnp.mean(x, -1, keepdims=True)
    centred = x - average
    rstd = lax.rsqrt(jnp.mean(centred * centred, -1, keepdims=True) + 1e-05)
    return centred * rstd, rstd


def norm_back(dy, gain, xhat, rstd):
    dx = dy * gain
    return rstd * (
        dx - jnp.mean(dx, -1, keepdims=True) - xhat * jnp.mean(dx * xhat, -1, keepdims=True)
    )


def per_head(fn, x):
    return [fn(x[h * TOK : (h + 1) * TOK], 0, keepdims=True) for h in range(3)]


def by_head(op, x, parts):
    return jnp.concatenate(
        [op(x[h * TOK : (h + 1) * TOK], parts[h]) for h in range(3)], 0
    )


def softmax(s):
    e = by_head(lambda x, top: jnp.exp(x - top), s, per_head(jnp.max, s))
    return by_head(lambda x, total: x * (1.0 / total), e, per_head(jnp.sum, e))


def head_masks(channels):
    lane = lax.broadcasted_iota(jnp.int32, (1, channels), 1)
    size = channels // 3
    return [((lane >= h * size) & (lane < (h + 1) * size)) for h in range(3)]


def stack_heads(x, masks):
    zero = jnp.zeros_like(x)
    return jnp.concatenate([jnp.where(m, x, zero) for m in masks], 0)


def fold_heads(x, masks):
    out = jnp.where(masks[0], x[:TOK], 0.0)
    for h in (1, 2):
        out = out + jnp.where(masks[h], x[h * TOK : (h + 1) * TOK], 0.0)
    return out


def factors(n_row, n_col):
    phases = [[("col", 1, 2)], [("col", 2, 2), ("row", 1, n_row)], [("col", 4, n_col // 4)]]
    phases = [[f for f in p if f[2] > 1] for p in phases]
    return [p for p in phases if p]


def kernel(
    n_row,
    n_col,
    units,
    region,
    cot,
    gains,
    wqkv,
    bqkv,
    xtab,
    wproj,
    wup,
    bup,
    wdown,
    out,
    grad_region,
    o_qkv,
    o_proj,
    o_up,
    o_down,
    o_small,
    ws,
    bias,
    f0,
    h0,
    f1,
    h1,
    dh1,
    g1,
    a_qkv,
    a_proj,
    a_up,
    a_down,
    a_vec,
    a_bup,
    a_bias,
    hs_row,
    hr_row,
    hs_col,
    hr_col,
    halo_send,
    halo_recv,
    pack,
    sq,
    sk,
    sv,
    sp,
    smix,
    sa,
    sx,
    sr,
    fx,
    fr,
    ff,
    fm,
    fs,
    *rest,
):
    rows, cols, channels = region.shape
    prow, pcol = rows + WIN, cols + WIN
    wide = pcol + WIN
    scale = (channels // 3) ** (-0.5)
    phases = factors(n_row, n_col)
    n_ph = len(phases)
    rs_recv = rest[:n_ph]
    rs_acc = rest[n_ph : 2 * n_ph]
    ag_buf = rest[2 * n_ph : 3 * n_ph]
    red_send, red_recv = rest[3 * n_ph :]
    index = {"row": lax.axis_index("row"), "col": lax.axis_index("col")}
    count = {"row": n_row, "col": n_col}

    def device(changes):
        where = dict(index)
        where.update(changes)
        return (where["row"], where["col"])

    def side(axis, step):
        n = count[axis]
        return device({axis: lax.rem(index[axis] + (step + n), n)})

    def members(phase):
        size = 1
        me = 0
        for _, stride, n in phase:
            size *= n
        partners = []
        digits = []
        for axis, stride, n in phase:
            digit = lax.rem(lax.div(index[axis], stride), n)
            digits.append(digit)
            me = me * n + digit
        for d in range(1, size):
            rest_d, ds = d, []
            for _, _, n in reversed(phase):
                ds.append(rest_d % n)
                rest_d //= n
            ds = ds[::-1]
            neg = 0
            member = 0
            changes = {}
            for (axis, stride, n), digit, step in zip(phase, digits, ds):
                neg = neg * n + (-step) % n
                other = lax.rem(digit + step, n)
                member = member * n + other
                changes[axis] = changes.get(axis, index[axis]) + (other - digit) * stride
            partners.append((d, neg, member, device(changes)))
        return size, me, partners

    groups = [members(p) for p in phases]

    barrier = pltpu.get_barrier_semaphore()
    greet = [side("col", -1), side("col", 1), side("row", -1), side("row", 1)]
    for _, _, partners in groups:
        greet += [p[3] for p in partners]
    for dev in greet:
        pl.semaphore_signal(barrier, inc=1, device_id=dev, device_id_type=MESH)

    for ref in (a_qkv, a_proj, a_up, a_down, a_vec, a_bup, a_bias, dh1, f1, pack):
        ref[...] = jnp.zeros(ref.shape, ref.dtype)
    for b in range(2):
        whole = wqkv[b].astype(F32)
        for t in range(3):
            ws[b, t] = whole[:, t * channels : (t + 1) * channels].astype(BF)
        for r in range(WIN):
            at = (WIN - 1 - r) * WIN
            for h in range(3):
                part = xtab[b, h][:, at : at + TOK]
                bias[b, h * TOK + r * WIN : h * TOK + (r + 1) * WIN, :] = jnp.concatenate(
                    [part, part], 1
                )
    f0[...] = region[...].astype(F32)
    masks = head_masks(channels)

    def qkv_of(u, b):
        xhat, rstd = norm(u)
        a = (xhat * gains[b, 0:1, :]).astype(BF)
        line = bqkv[b : b + 1, :]
        parts = [
            (dot_nn(a, ws[b, t]) + line[:, t * channels : (t + 1) * channels]).astype(BF)
            for t in range(3)
        ]
        return xhat, rstd, a, parts

    def split(x, w):
        return x[w * TOK : (w + 1) * TOK]

    left = lax.broadcasted_iota(jnp.int32, (3 * TOK, 2 * TOK), 1) < TOK

    def pair_product(first, second, both):
        return jnp.where(left, dot_nt(first, both), dot_nt(second, both))

    def pair_rows(x, first, second):
        return jnp.concatenate([dot_tn(x, first)[:TOK], dot_tn(x, second)[TOK:]], 0)

    def pair_sum(x, both):
        rest_rows = jnp.zeros_like(both[:TOK])
        one = dot_nn(x, jnp.concatenate([both[:TOK], rest_rows], 0))
        two = dot_nn(x, jnp.concatenate([rest_rows, both[TOK:]], 0))
        return [fold_heads(one, masks), fold_heads(two, masks)]

    def stacked(x, w):
        return stack_heads(split(x, w), masks), stack_heads(split(x, w + 1), masks)

    def attn_forward(u, b, at, usable):
        xhat, rstd, a, (q, k, v) = qkv_of(u, b)
        sq[at], sk[at], sv[at], sa[at] = q, k, v, a
        sx[at] = xhat
        sr[at] = jnp.broadcast_to(rstd, xhat.shape)
        mixed = []
        for w in range(0, GROUP, 2):
            both = q[w * TOK : (w + 2) * TOK]
            s = pair_product(*stacked(k, w), both) * scale + bias[b]
            if usable is not None:
                s = jnp.where(usable(w), s, -1e30)
            p = softmax(s)
            sp[at, w // 2] = p
            mixed.append(pair_rows(p.astype(BF), *stacked(v, w)))
        mixed = jnp.concatenate(mixed, 0).astype(BF)
        smix[at] = mixed
        return u + dot_nn(mixed, wproj[b])

    def attn_backward(dh, b, at):
        xhat, rstd, a, q, k, v = sx[at], sr[at], sa[at], sq[at], sk[at], sv[at]
        dhb = dh.astype(BF)
        dmix = dot_nt(dhb, wproj[b]).astype(BF)
        a_proj[b] += dot_tn(smix[at], dhb)
        dqs, dks, dvs = [], [], []
        dbias = None
        for w in range(0, GROUP, 2):
            both, do = q[w * TOK : (w + 2) * TOK], dmix[w * TOK : (w + 2) * TOK]
            p = sp[at, w // 2]
            dp = pair_product(*stacked(v, w), do)
            ds = p * by_head(jnp.subtract, dp, per_head(jnp.sum, dp * p))
            dbias = ds if dbias is None else dbias + ds
            dsb = (ds * scale).astype(BF)
            dqs.append(pair_rows(dsb, *stacked(k, w)))
            dks += pair_sum(dsb, both)
            dvs += pair_sum(p.astype(BF), do)
        a_bias[b] += dbias
        da = None
        for t, parts in enumerate((dqs, dks, dvs)):
            grad = jnp.concatenate(parts, 0)
            a_vec[b, t : t + 1, :] += jnp.sum(grad, 0, keepdims=True)
            grad = grad.astype(BF)
            a_qkv[b, t] += dot_tn(a, grad)
            term = dot_nt(grad, ws[b, t])
            da = term if da is None else da + term
        a_vec[b, 3:4, :] += jnp.sum(da * xhat, 0, keepdims=True)
        return dh + norm_back(da, gains[b, 0:1, :], xhat, rstd)

    def gelu(z):
        t = jnp.tanh(0.7978845608028654 * z * (1.0 + 0.044715 * z * z))
        return t, 0.5 * z * (1.0 + t)

    def slope_of(z, t):
        return 0.5 * (1.0 + t) + 0.5 * z * (1.0 - t * t) * (
            0.7978845608028654 * (1.0 + 0.134145 * z * z)
        )

    def feed_forward(h, b):
        xhat, rstd = norm(h)
        f = (xhat * gains[b, 1:2, :]).astype(BF)
        z = dot_nn(f, wup[b]) + bup[b : b + 1, :]
        t, m = gelu(z)
        m = m.astype(BF)
        return h + dot_nt(m, wdown[b]), (xhat, rstd, f, m, slope_of(z, t))

    def feed_backward(saved, g, b):
        xhat, rstd, f, m, slope = saved
        gb = g.astype(BF)
        dz = dot_nn(gb, wdown[b]) * slope
        a_bup[b : b + 1, :] += jnp.sum(dz, 0, keepdims=True)
        dz = dz.astype(BF)
        a_down[b] += dot_tn(gb, m)
        a_up[b] += dot_tn(f, dz)
        df = dot_nt(dz, wup[b])
        a_vec[b, 4:5, :] += jnp.sum(df * xhat, 0, keepdims=True)
        return g + norm_back(df, gains[b, 1:2, :], xhat, rstd)

    def spots0(j):
        return [
            (i * WIN, pl.multiple_of((j * 3 + c) * WIN, WIN))
            for i in range(rows // WIN)
            for c in range(3)
        ]

    def spots1(j):
        return [
            (i * WIN, pl.multiple_of((j * 2 + c) * WIN, WIN))
            for i in range(prow // WIN)
            for c in range(2)
        ]

    def gather(ref, spots):
        return jnp.concatenate(
            [ref[r : r + WIN, pl.ds(c, WIN), :].reshape(TOK, channels) for r, c in spots], 0
        )

    def scatter(ref, spots, x):
        for w, (r, c) in enumerate(spots):
            ref[r : r + WIN, pl.ds(c, WIN), :] = split(x, w).reshape(WIN, WIN, channels)

    key = lax.broadcasted_iota(jnp.int32, (3 * TOK, 2 * TOK), 0)
    key_row = lax.div(lax.rem(key, TOK), WIN) + (index["row"] * rows - HALF)
    key_col = lax.rem(key, WIN) + jnp.where(left, 0, WIN) + (index["col"] * cols - HALF)

    def usable1(j):
        def usable(w):
            row = key_row + (w // 2) * WIN
            col = key_col + j * (2 * WIN)
            return (row >= 0) & (row < n_row * rows) & (col >= 0) & (col < n_col * cols)

        return usable

    n0 = cols // (3 * WIN)
    n1 = wide // (2 * WIN)
    strip = 4
    flat = strip * cols

    @pl.loop(0, n0)
    def _(j):
        spots = spots0(j)
        scatter(h0, spots, attn_forward(gather(f0, spots), 0, j, None))

    @pl.loop(0, rows // strip)
    def _(j):
        h = h0[pl.ds(j * strip, strip)].reshape(flat, channels)
        low, (xhat, rstd, f, m, slope) = feed_forward(h, 0)
        fx[j], ff[j], fm[j], fs[j] = xhat, f, m, slope
        fr[j] = jnp.broadcast_to(rstd, xhat.shape)
        low = low.astype(BF).astype(F32)
        f1[pl.ds(HALF + j * strip, strip), HALF : HALF + cols, :] = low.reshape(
            strip, cols, channels
        )

    def exchange(slot, axis, sends, recvs):
        copies = []
        for way, (step, there) in enumerate(((-1, 1), (1, 0))):
            copy = pltpu.make_async_remote_copy(
                src_ref=sends.at[slot // 2, way],
                dst_ref=recvs.at[slot // 2, there],
                send_sem=halo_send.at[2 * slot + way],
                recv_sem=halo_recv.at[2 * slot + there],
                device_id=side(axis, step),
                device_id_type=MESH,
            )
            copy.start()
            copies.append(copy)
        for copy in copies:
            copy.wait()

    pl.semaphore_wait(barrier, len(greet))

    def put_rows(at, field, first, second):
        hs_row[at, 0] = field[first : first + HALF, 0:pcol, :].reshape(HALF * pcol, channels).astype(BF)
        hs_row[at, 1] = field[second : second + HALF, 0:pcol, :].reshape(HALF * pcol, channels).astype(BF)

    def put_cols(at, field):
        hs_col[at, 0] = field[:, 0:WIN, :].reshape(prow * WIN, channels).astype(BF)
        hs_col[at, 1] = field[:, pcol - WIN : pcol, :].reshape(prow * WIN, channels).astype(BF)

    def got_row(at, way):
        return hr_row[at, way].astype(F32).reshape(HALF, pcol, channels)

    def got_col(at, way):
        return hr_col[at, way].astype(F32).reshape(prow, WIN, channels)

    put_rows(0, f1, HALF, rows)
    exchange(0, "row", hs_row, hr_row)
    f1[0:HALF, 0:pcol, :] = got_row(0, 0)
    f1[prow - HALF : prow, 0:pcol, :] = got_row(0, 1)
    put_cols(0, f1)
    exchange(1, "col", hs_col, hr_col)
    upper_half = lax.broadcasted_iota(jnp.int32, (prow, WIN, channels), 1) >= HALF
    f1[:, 0:WIN, :] = jnp.where(upper_half, f1[:, 0:WIN, :], got_col(0, 0))
    f1[:, pcol - WIN : pcol, :] = jnp.where(
        upper_half, got_col(0, 1), f1[:, pcol - WIN : pcol, :]
    )

    @pl.loop(0, n1)
    def _(j):
        spots = spots1(j)
        scatter(h1, spots, attn_forward(gather(f1, spots), 1, n0 + j, usable1(j)))

    @pl.loop(0, rows // strip)
    def _(j):
        inner = pl.ds(HALF + j * strip, strip)
        h = h1[inner, HALF : HALF + cols, :].reshape(flat, channels)
        g = cot[pl.ds(j * strip, strip)].astype(F32).reshape(flat, channels)
        result, saved = feed_forward(h, 1)
        dh = feed_backward(saved, g, 1)
        out[pl.ds(j * strip, strip)] = result.reshape(strip, cols, channels).astype(BF)
        dh1[inner, HALF : HALF + cols, :] = dh.reshape(strip, cols, channels)

    @pl.loop(0, n1)
    def _(j):
        spots = spots1(j)
        scatter(g1, spots, attn_backward(gather(dh1, spots), 1, n0 + j))

    put_cols(1, g1)
    exchange(3, "col", hs_col, hr_col)
    g1[:, 0:WIN, :] += got_col(1, 0)
    g1[:, pcol - WIN : pcol, :] += got_col(1, 1)
    put_rows(1, g1, 0, prow - HALF)
    exchange(2, "row", hs_row, hr_row)
    g1[HALF : 2 * HALF, 0:pcol, :] += got_row(1, 0)
    g1[rows : rows + HALF, 0:pcol, :] += got_row(1, 1)

    @pl.loop(0, rows // strip)
    def _(j):
        here = pl.ds(j * strip, strip)
        g = g1[pl.ds(HALF + j * strip, strip), HALF : HALF + cols, :].reshape(flat, channels)
        dh = feed_backward((fx[j], fr[j], ff[j], fm[j], fs[j]), g, 0)
        h0[here] = dh.reshape(strip, cols, channels)

    @pl.loop(0, n0)
    def _(j):
        spots = spots0(j)
        scatter(grad_region, spots, attn_backward(gather(h0, spots), 0, j))

    def stow(unit, x, width):
        n = x.shape[0] // 16
        for t in range((width + 127) // 128):
            part = x[:, t * 128 : min(width, (t + 1) * 128)]
            wide = part.shape[1]
            pack[unit + t * n : unit + (t + 1) * n, :, 0:wide] = part.reshape(n, 16, wide).astype(BF)

    hidden = wup.shape[2]
    for b in range(2):
        base = b * U_BLOCK
        for t in range(3):
            stow(base + U_QKV + 6 * t, a_qkv[b, t], channels)
        stow(base + U_PROJ, a_proj[b], channels)
        stow(base + U_UP, a_up[b], hidden)
        stow(base + U_DOWN, a_down[b], hidden)
        heads = []
        for h in range(3):
            total = None
            for r in range(WIN):
                at = (WIN - 1 - r) * WIN
                line = h * TOK + r * WIN
                part = a_bias[b, line : line + WIN, :]
                part = part[:, :TOK] + part[:, TOK:]
                pieces = [part, jnp.zeros((WIN, 128 - at - TOK), F32)]
                if at:
                    pieces = [jnp.zeros((WIN, at), F32)] + pieces
                part = jnp.concatenate(pieces, 1)
                total = part if total is None else total + part
            heads.append(total)
        vec = jnp.concatenate([a_vec[b], jnp.zeros((WIN, 128 - channels), F32)], 1)
        sub = lax.broadcasted_iota(jnp.int32, (WIN, 128), 0)
        for t in range(3):
            vec = jnp.where(sub == 5 + t, a_bup[b : b + 1, t * 128 : (t + 1) * 128], vec)
        small = jnp.concatenate([vec] + heads, 0)
        stow(base + U_SMALL, small, 128)

    source = pack
    size_now = units
    at_sem = 0
    for ph, (size, me, partners) in enumerate(groups):
        part = size_now // size
        copies = []
        for d, neg, member, dev in partners:
            copy = pltpu.make_async_remote_copy(
                src_ref=source.at[pl.ds(member * part, part)],
                dst_ref=rs_recv[ph].at[neg - 1],
                send_sem=red_send.at[at_sem + d - 1],
                recv_sem=red_recv.at[at_sem + neg - 1],
                device_id=dev,
                device_id_type=MESH,
            )
            copy.start()
            copies.append(copy)
        total = source[pl.ds(me * part, part)].astype(F32)
        for copy in copies:
            copy.wait()
        for d in range(size - 1):
            total = total + rs_recv[ph][d].astype(F32)
        rs_acc[ph][...] = total.astype(BF)
        source = rs_acc[ph]
        size_now = part
        at_sem += size - 1
    for ph in reversed(range(n_ph)):
        size, me, partners = groups[ph]
        part = size_now
        copies = []
        for d, neg, member, dev in partners:
            copy = pltpu.make_async_remote_copy(
                src_ref=source,
                dst_ref=ag_buf[ph].at[pl.ds(me * part, part)],
                send_sem=red_send.at[at_sem + d - 1],
                recv_sem=red_recv.at[at_sem + neg - 1],
                device_id=dev,
                device_id_type=MESH,
            )
            copy.start()
            copies.append(copy)
        ag_buf[ph][pl.ds(me * part, part)] = source[...]
        for copy in copies:
            copy.wait()
        source = ag_buf[ph]
        size_now = part * size
        at_sem += size - 1

    def fetch(unit, n, width=128):
        return source[unit : unit + n].astype(F32).reshape(n * 16, 128)[:, :width]

    for b in range(2):
        base = b * U_BLOCK
        for t in range(3):
            o_qkv[b, t] = fetch(base + U_QKV + 6 * t, 6, channels)
            o_up[b, :, t * 128 : (t + 1) * 128] = fetch(base + U_UP + 6 * t, 6)
            o_down[b, :, t * 128 : (t + 1) * 128] = fetch(base + U_DOWN + 6 * t, 6)
        o_proj[b] = fetch(base + U_PROJ, 6, channels)
        o_small[b] = fetch(base + U_SMALL, 2)


def expand_table(table):
    side = 2 * WIN - 1
    grid = table.reshape(2, -1, side, side)
    x = jnp.stack([grid[..., WIN - 1 - c : side - c] for c in range(WIN)], 2)
    return x.reshape(2, grid.shape[1], WIN, side * WIN)


def fold_table(dx):
    side = 2 * WIN - 1
    x = dx.reshape(2, -1, WIN, side, WIN)
    total = 0.0
    for c in range(WIN):
        total = total + jnp.pad(
            x[:, :, c], ((0, 0), (0, 0), (0, 0), (WIN - 1 - c, c))
        )
    return total.reshape(2, -1, side * side)


def body(n_row, n_col, region, cotangent, gains, wqkv, bqkv, table, wproj, wup, bup, wdown):
    rows, cols, channels = region.shape
    hidden = wup.shape[2]
    prow, pcol = rows + WIN, cols + WIN
    devices = n_row * n_col
    units = -(-2 * U_BLOCK // devices) * devices
    phases = factors(n_row, n_col)
    sizes = []
    for phase in phases:
        size = 1
        for f in phase:
            size *= f[2]
        sizes.append(size)
    recv, acc, gath = [], [], []
    now = units
    for size in sizes:
        gath.append(pltpu.VMEM((now, 16, 128), BF))
        now //= size
        recv.append(pltpu.VMEM((size - 1, now, 16, 128), BF))
        acc.append(pltpu.VMEM((now, 16, 128), BF))
    turns = cols // (3 * WIN) + (pcol + WIN) // (2 * WIN)
    steps = 2 * sum(s - 1 for s in sizes)
    vmem = pl.BlockSpec(memory_space=pltpu.VMEM)
    shapes = [
        jax.ShapeDtypeStruct((rows, cols, channels), BF),
        jax.ShapeDtypeStruct((rows, cols, channels), F32),
        jax.ShapeDtypeStruct((2, 3, channels, channels), F32),
        jax.ShapeDtypeStruct((2, channels, channels), F32),
        jax.ShapeDtypeStruct((2, channels, hidden), F32),
        jax.ShapeDtypeStruct((2, channels, hidden), F32),
        jax.ShapeDtypeStruct((2, 32, 128), F32),
    ]
    field0 = pltpu.VMEM((rows, cols, channels), F32)
    field1 = pltpu.VMEM((prow, pcol + WIN, channels), F32)
    results = pl.pallas_call(
        functools.partial(kernel, n_row, n_col, units),
        out_shape=shapes,
        in_specs=[vmem] * 10,
        out_specs=[vmem] * len(shapes),
        scratch_shapes=[
            pltpu.VMEM((2, 3, channels, channels), BF),
            pltpu.VMEM((2, 3 * TOK, 2 * TOK), F32),
            field0,
            field0,
            field1,
            field1,
            field1,
            field1,
            pltpu.VMEM((2, 3, channels, channels), F32),
            pltpu.VMEM((2, channels, channels), F32),
            pltpu.VMEM((2, channels, hidden), F32),
            pltpu.VMEM((2, channels, hidden), F32),
            pltpu.VMEM((2, 8, channels), F32),
            pltpu.VMEM((2, hidden), F32),
            pltpu.VMEM((2, 3 * TOK, 2 * TOK), F32),
            pltpu.VMEM((2, 2, HALF * pcol, channels), BF),
            pltpu.VMEM((2, 2, HALF * pcol, channels), BF),
            pltpu.VMEM((2, 2, prow * WIN, channels), BF),
            pltpu.VMEM((2, 2, prow * WIN, channels), BF),
            pltpu.SemaphoreType.DMA((8,)),
            pltpu.SemaphoreType.DMA((8,)),
            pltpu.VMEM((units, 16, 128), BF),
            *[pltpu.VMEM((turns, GROUP * TOK, channels), BF)] * 3,
            pltpu.VMEM((turns, GROUP // 2, 3 * TOK, 2 * TOK), F32),
            *[pltpu.VMEM((turns, GROUP * TOK, channels), BF)] * 2,
            *[pltpu.VMEM((turns, GROUP * TOK, channels), F32)] * 2,
            *[pltpu.VMEM((rows // 4, 4 * cols, channels), F32)] * 2,
            pltpu.VMEM((rows // 4, 4 * cols, channels), BF),
            pltpu.VMEM((rows // 4, 4 * cols, hidden), BF),
            pltpu.VMEM((rows // 4, 4 * cols, hidden), F32),
            *recv,
            *acc,
            *gath,
            pltpu.SemaphoreType.DMA((steps,)),
            pltpu.SemaphoreType.DMA((steps,)),
        ],
        compiler_params=pltpu.CompilerParams(
            collective_id=0, has_side_effects=True, vmem_limit_bytes=48 * 1024 * 1024
        ),
        name="swin_pair",
    )(region, cotangent, gains, wqkv, bqkv, expand_table(table), wproj, wup, bup, wdown.transpose(0, 2, 1))
    out, grad_region, dqkv, dproj, dup, down_t, small = results
    vec = small[:, 0:5, :channels]
    return (
        out,
        grad_region,
        vec[:, 3:5],
        dqkv.transpose(0, 2, 1, 3).reshape(2, channels, 3 * channels),
        vec[:, 0:3].reshape(2, 3 * channels),
        fold_table(small[:, 8:32, : (2 * WIN - 1) * WIN].reshape(2, 3, WIN, -1)),
        dproj,
        dup,
        small[:, 5:8].reshape(2, hidden),
        down_t.transpose(0, 2, 1),
    )


def solution(mesh):
    tile = P("row", "col", None)
    return jax.shard_map(
        functools.partial(body, mesh.shape["row"], mesh.shape["col"]),
        mesh=mesh,
        in_specs=(tile, tile) + (P(),) * 8,
        out_specs=(tile, tile) + (P(),) * 8,
        check_vma=False,
    )
```

```python
import functools

import jax
import jax.numpy as jnp
from jax import lax
from jax.experimental import pallas as pl
from jax.experimental.pallas import tpu as pltpu
from jax.sharding import PartitionSpec as P

WIN = 8
HALF = 4
TOK = 64
BF = jnp.bfloat16
F32 = jnp.float32
MESH = pl.DeviceIdType.MESH
GROUP = 6

U_QKV = 0
U_PROJ = 18
U_UP = 24
U_DOWN = 42
U_SMALL = 60
U_BLOCK = 62


def dot_nn(a, b):
    return lax.dot_general(a, b, (((1,), (0,)), ((), ())), preferred_element_type=F32)


def dot_nt(a, b):
    return lax.dot_general(a, b, (((1,), (1,)), ((), ())), preferred_element_type=F32)


def dot_tn(a, b):
    return lax.dot_general(a, b, (((0,), (0,)), ((), ())), preferred_element_type=F32)


def norm(x):
    average = jnp.mean(x, -1, keepdims=True)
    centred = x - average
    rstd = lax.rsqrt(jnp.mean(centred * centred, -1, keepdims=True) + 1e-05)
    return centred * rstd, rstd


def norm_back(dy, gain, xhat, rstd):
    dx = dy * gain
    return rstd * (
        dx - jnp.mean(dx, -1, keepdims=True) - xhat * jnp.mean(dx * xhat, -1, keepdims=True)
    )


def per_head(fn, x):
    return [fn(x[h * TOK : (h + 1) * TOK], 0, keepdims=True) for h in range(3)]


def by_head(op, x, parts):
    return jnp.concatenate(
        [op(x[h * TOK : (h + 1) * TOK], parts[h]) for h in range(3)], 0
    )


def softmax(s):
    e = by_head(lambda x, top: jnp.exp(x - top), s, per_head(jnp.max, s))
    return by_head(lambda x, total: x * (1.0 / total), e, per_head(jnp.sum, e))


def head_masks(channels):
    lane = lax.broadcasted_iota(jnp.int32, (1, channels), 1)
    size = channels // 3
    return [((lane >= h * size) & (lane < (h + 1) * size)) for h in range(3)]


def stack_heads(x, masks):
    zero = jnp.zeros_like(x)
    return jnp.concatenate([jnp.where(m, x, zero) for m in masks], 0)


def fold_heads(x, masks):
    out = jnp.where(masks[0], x[:TOK], 0.0)
    for h in (1, 2):
        out = out + jnp.where(masks[h], x[h * TOK : (h + 1) * TOK], 0.0)
    return out


def offsets(c):
    side = 2 * WIN - 1
    shape = (side * side, 128)
    lane = lax.broadcasted_iota(jnp.int32, shape, 1)
    entry = lax.broadcasted_iota(jnp.int32, shape, 0)
    wanted = lax.div(lane, WIN) * side + lax.rem(lane, WIN) + (WIN - 1 - c)
    return jnp.where((entry == wanted) & (lane < side * WIN), 1.0, 0.0).astype(BF)


def factors(n_row, n_col):
    phases = [[("col", 1, 2)], [("col", 2, 2), ("row", 1, n_row)], [("col", 4, n_col // 4)]]
    phases = [[f for f in p if f[2] > 1] for p in phases]
    return [p for p in phases if p]


def kernel(
    n_row,
    n_col,
    units,
    region,
    cot,
    gains,
    wqkv,
    bqkv,
    table,
    wproj,
    wup,
    bup,
    wdown,
    out,
    grad_region,
    o_low,
    o_high,
    ws,
    xtab,
    bias,
    f0,
    h0,
    f1,
    h1,
    dh1,
    g1,
    a_qkv,
    a_proj,
    a_up,
    a_down,
    a_vec,
    a_bup,
    a_bias,
    hs_row,
    hr_row,
    hs_col,
    hr_col,
    halo_send,
    halo_recv,
    pack,
    sq,
    sk,
    sv,
    sp,
    smix,
    sa,
    sx,
    sr,
    fx,
    fr,
    ff,
    fm,
    fs,
    *rest,
):
    rows, cols, channels = region.shape
    prow, pcol = rows + WIN, cols + WIN
    wide = pcol + WIN
    scale = (channels // 3) ** (-0.5)
    phases = factors(n_row, n_col)
    n_ph = len(phases)
    rs_recv = rest[:n_ph]
    rs_acc = rest[n_ph : 2 * n_ph]
    ag_buf = rest[2 * n_ph : 3 * n_ph]
    red_send, red_recv = rest[3 * n_ph :]
    index = {"row": lax.axis_index("row"), "col": lax.axis_index("col")}
    count = {"row": n_row, "col": n_col}

    def device(changes):
        where = dict(index)
        where.update(changes)
        return (where["row"], where["col"])

    def side(axis, step):
        n = count[axis]
        return device({axis: lax.rem(index[axis] + (step + n), n)})

    def members(phase):
        size = 1
        me = 0
        for _, stride, n in phase:
            size *= n
        partners = []
        digits = []
        for axis, stride, n in phase:
            digit = lax.rem(lax.div(index[axis], stride), n)
            digits.append(digit)
            me = me * n + digit
        for d in range(1, size):
            rest_d, ds = d, []
            for _, _, n in reversed(phase):
                ds.append(rest_d % n)
                rest_d //= n
            ds = ds[::-1]
            neg = 0
            member = 0
            changes = {}
            for (axis, stride, n), digit, step in zip(phase, digits, ds):
                neg = neg * n + (-step) % n
                other = lax.rem(digit + step, n)
                member = member * n + other
                changes[axis] = changes.get(axis, index[axis]) + (other - digit) * stride
            partners.append((d, neg, member, device(changes)))
        return size, me, partners

    groups = [members(p) for p in phases]

    barrier = pltpu.get_barrier_semaphore()
    greet = [side("col", -1), side("col", 1), side("row", -1), side("row", 1)]
    for _, _, partners in groups:
        greet += [p[3] for p in partners]
    for dev in greet:
        pl.semaphore_signal(barrier, inc=1, device_id=dev, device_id_type=MESH)

    for ref in (a_qkv, a_proj, a_up, a_down, a_vec, a_bup, a_bias, dh1, f1, pack):
        ref[...] = jnp.zeros(ref.shape, ref.dtype)
    terms = []
    left_over = table[...].reshape(6, table.shape[2])
    for _ in range(3):
        terms.append(left_over.astype(BF))
        left_over = left_over - terms[-1].astype(F32)
    for c in range(WIN):
        hot = offsets(c)
        line = dot_nn(terms[0], hot) + dot_nn(terms[1], hot) + dot_nn(terms[2], hot)
        for n in range(6):
            xtab[n // 3, n % 3, c : c + 1, :] = line[n : n + 1]
    for b in range(2):
        whole = wqkv[b].astype(F32)
        for t in range(3):
            ws[b, t] = whole[:, t * channels : (t + 1) * channels].astype(BF)
        for r in range(WIN):
            at = (WIN - 1 - r) * WIN
            for h in range(3):
                part = xtab[b, h][:, at : at + TOK]
                bias[b, h * TOK + r * WIN : h * TOK + (r + 1) * WIN, :] = jnp.concatenate(
                    [part, part], 1
                )
    f0[...] = region[...].astype(F32)
    masks = head_masks(channels)

    def qkv_of(u, b):
        xhat, rstd = norm(u)
        a = (xhat * gains[b, 0:1, :]).astype(BF)
        line = bqkv[b : b + 1, :]
        parts = [
            (dot_nn(a, ws[b, t]) + line[:, t * channels : (t + 1) * channels]).astype(BF)
            for t in range(3)
        ]
        return xhat, rstd, a, parts

    def split(x, w):
        return x[w * TOK : (w + 1) * TOK]

    left = lax.broadcasted_iota(jnp.int32, (3 * TOK, 2 * TOK), 1) < TOK

    def pair_product(first, second, both):
        return jnp.where(left, dot_nt(first, both), dot_nt(second, both))

    def pair_rows(x, first, second):
        return jnp.concatenate([dot_tn(x, first)[:TOK], dot_tn(x, second)[TOK:]], 0)

    def pair_sum(x, both):
        rest_rows = jnp.zeros_like(both[:TOK])
        one = dot_nn(x, jnp.concatenate([both[:TOK], rest_rows], 0))
        two = dot_nn(x, jnp.concatenate([rest_rows, both[TOK:]], 0))
        return [fold_heads(one, masks), fold_heads(two, masks)]

    def stacked(x, w):
        return stack_heads(split(x, w), masks), stack_heads(split(x, w + 1), masks)

    def attn_forward(u, b, at, usable):
        xhat, rstd, a, (q, k, v) = qkv_of(u, b)
        sq[at], sk[at], sv[at], sa[at] = q, k, v, a
        sx[at] = xhat
        sr[at] = jnp.broadcast_to(rstd, xhat.shape)
        mixed = []
        for w in range(0, GROUP, 2):
            both = q[w * TOK : (w + 2) * TOK]
            s = pair_product(*stacked(k, w), both) * scale + bias[b]
            if usable is not None:
                s = jnp.where(usable(w), s, -1e30)
            p = softmax(s)
            sp[at, w // 2] = p
            mixed.append(pair_rows(p.astype(BF), *stacked(v, w)))
        mixed = jnp.concatenate(mixed, 0).astype(BF)
        smix[at] = mixed
        return u + dot_nn(mixed, wproj[b])

    def attn_backward(dh, b, at):
        xhat, rstd, a, q, k, v = sx[at], sr[at], sa[at], sq[at], sk[at], sv[at]
        dhb = dh.astype(BF)
        dmix = dot_nt(dhb, wproj[b]).astype(BF)
        a_proj[b] += dot_tn(smix[at], dhb)
        dqs, dks, dvs = [], [], []
        dbias = None
        for w in range(0, GROUP, 2):
            both, do = q[w * TOK : (w + 2) * TOK], dmix[w * TOK : (w + 2) * TOK]
            p = sp[at, w // 2]
            dp = pair_product(*stacked(v, w), do)
            ds = p * by_head(jnp.subtract, dp, per_head(jnp.sum, dp * p))
            dbias = ds if dbias is None else dbias + ds
            dsb = (ds * scale).astype(BF)
            dqs.append(pair_rows(dsb, *stacked(k, w)))
            dks += pair_sum(dsb, both)
            dvs += pair_sum(p.astype(BF), do)
        a_bias[b] += dbias
        da = None
        for t, parts in enumerate((dqs, dks, dvs)):
            grad = jnp.concatenate(parts, 0)
            a_vec[b, t : t + 1, :] += jnp.sum(grad, 0, keepdims=True)
            grad = grad.astype(BF)
            a_qkv[b, t] += dot_tn(a, grad)
            term = dot_nt(grad, ws[b, t])
            da = term if da is None else da + term
        a_vec[b, 3:4, :] += jnp.sum(da * xhat, 0, keepdims=True)
        return dh + norm_back(da, gains[b, 0:1, :], xhat, rstd)

    def gelu(z):
        t = jnp.tanh(0.7978845608028654 * z * (1.0 + 0.044715 * z * z))
        return t, 0.5 * z * (1.0 + t)

    def slope_of(z, t):
        return 0.5 * (1.0 + t) + 0.5 * z * (1.0 - t * t) * (
            0.7978845608028654 * (1.0 + 0.134145 * z * z)
        )

    def feed_forward(h, b):
        xhat, rstd = norm(h)
        f = (xhat * gains[b, 1:2, :]).astype(BF)
        z = dot_nn(f, wup[b]) + bup[b : b + 1, :]
        t, m = gelu(z)
        m = m.astype(BF)
        return h + dot_nt(m, wdown[b]), (xhat, rstd, f, m, slope_of(z, t))

    def feed_backward(saved, g, b):
        xhat, rstd, f, m, slope = saved
        gb = g.astype(BF)
        dz = dot_nn(gb, wdown[b]) * slope
        a_bup[b : b + 1, :] += jnp.sum(dz, 0, keepdims=True)
        dz = dz.astype(BF)
        a_down[b] += dot_tn(gb, m)
        a_up[b] += dot_tn(f, dz)
        df = dot_nt(dz, wup[b])
        a_vec[b, 4:5, :] += jnp.sum(df * xhat, 0, keepdims=True)
        return g + norm_back(df, gains[b, 1:2, :], xhat, rstd)

    def spots0(j):
        return [
            (i * WIN, (j * 3 + c) * WIN)
            for i in range(rows // WIN)
            for c in range(3)
        ]

    def spots1(j):
        return [
            (i * WIN, (j * 2 + c) * WIN)
            for i in range(prow // WIN)
            for c in range(2)
        ]

    def gather(ref, spots):
        return jnp.concatenate(
            [ref[r : r + WIN, pl.ds(c, WIN), :].reshape(TOK, channels) for r, c in spots], 0
        )

    def scatter(ref, spots, x):
        for w, (r, c) in enumerate(spots):
            ref[r : r + WIN, pl.ds(c, WIN), :] = split(x, w).reshape(WIN, WIN, channels)

    key = lax.broadcasted_iota(jnp.int32, (3 * TOK, 2 * TOK), 0)
    key_row = lax.div(lax.rem(key, TOK), WIN) + (index["row"] * rows - HALF)
    key_col = lax.rem(key, WIN) + jnp.where(left, 0, WIN) + (index["col"] * cols - HALF)

    def usable1(j):
        def usable(w):
            row = key_row + (w // 2) * WIN
            col = key_col + j * (2 * WIN)
            return (row >= 0) & (row < n_row * rows) & (col >= 0) & (col < n_col * cols)

        return usable

    n0 = cols // (3 * WIN)
    n1 = wide // (2 * WIN)
    strip = 4
    flat = strip * cols

    def stow(b, unit, x, width):
        n = x.shape[0] // 16
        for t in range((width + 127) // 128):
            part = x[:, t * 128 : min(width, (t + 1) * 128)]
            wide = part.shape[1]
            pack[b, unit + t * n : unit + (t + 1) * n, :, 0:wide] = part.reshape(n, 16, wide).astype(BF)

    hidden = wup.shape[2]
    def pack_grads(b):
        for t in range(3):
            stow(b, U_QKV + 6 * t, a_qkv[b, t], channels)
        stow(b, U_PROJ, a_proj[b], channels)
        stow(b, U_UP, a_up[b], hidden)
        stow(b, U_DOWN, a_down[b], hidden)
        heads = []
        for h in range(3):
            total = None
            for r in range(WIN):
                at = (WIN - 1 - r) * WIN
                line = h * TOK + r * WIN
                part = a_bias[b, line : line + WIN, :]
                part = part[:, :TOK] + part[:, TOK:]
                pieces = [part, jnp.zeros((WIN, 128 - at - TOK), F32)]
                if at:
                    pieces = [jnp.zeros((WIN, at), F32)] + pieces
                part = jnp.concatenate(pieces, 1)
                total = part if total is None else total + part
            heads.append(total)
        vec = jnp.concatenate([a_vec[b], jnp.zeros((WIN, 128 - channels), F32)], 1)
        sub = lax.broadcasted_iota(jnp.int32, (WIN, 128), 0)
        for t in range(3):
            vec = jnp.where(sub == 5 + t, a_bup[b : b + 1, t * 128 : (t + 1) * 128], vec)
        small = jnp.concatenate([vec] + heads, 0)
        stow(b, U_SMALL, small, 128)

    def reduce_steps(b):
        source = pack.at[b]
        size_now = units
        at_sem = 0
        for ph, (size, me, partners) in enumerate(groups):
            part = size_now // size
            copies = []
            for d, neg, member, dev in partners:
                copy = pltpu.make_async_remote_copy(
                    src_ref=source.at[pl.ds(member * part, part)],
                    dst_ref=rs_recv[ph].at[b, neg - 1],
                    send_sem=red_send.at[b, at_sem + d - 1],
                    recv_sem=red_recv.at[b, at_sem + neg - 1],
                    device_id=dev,
                    device_id_type=MESH,
                )
                copy.start()
                copies.append(copy)
            yield
            total = source[pl.ds(me * part, part)].astype(F32)
            for copy in copies:
                copy.wait()
            for d in range(size - 1):
                total = total + rs_recv[ph][b, d].astype(F32)
            rs_acc[ph][b] = total.astype(BF)
            source = rs_acc[ph].at[b]
            size_now = part
            at_sem += size - 1
        for ph in reversed(range(n_ph)):
            size, me, partners = groups[ph]
            part = size_now
            copies = []
            for d, neg, member, dev in partners:
                copy = pltpu.make_async_remote_copy(
                    src_ref=source,
                    dst_ref=ag_buf[ph].at[b, pl.ds(me * part, part)],
                    send_sem=red_send.at[b, at_sem + d - 1],
                    recv_sem=red_recv.at[b, at_sem + neg - 1],
                    device_id=dev,
                    device_id_type=MESH,
                )
                copy.start()
                copies.append(copy)
            ag_buf[ph][b, pl.ds(me * part, part)] = source[...]
            yield
            for copy in copies:
                copy.wait()
            source = ag_buf[ph].at[b]
            size_now = part * size
            at_sem += size - 1
        (o_low, o_high)[b][...] = source[...]

    for j in range(n0):
        spots = spots0(j)
        scatter(h0, spots, attn_forward(gather(f0, spots), 0, j, None))

    for j in range(rows // strip):
        h = h0[pl.ds(j * strip, strip)].reshape(flat, channels)
        low, (xhat, rstd, f, m, slope) = feed_forward(h, 0)
        fx[j], ff[j], fm[j], fs[j] = xhat, f, m, slope
        fr[j] = jnp.broadcast_to(rstd, xhat.shape)
        low = low.astype(BF).astype(F32)
        f1[pl.ds(HALF + j * strip, strip), HALF : HALF + cols, :] = low.reshape(
            strip, cols, channels
        )

    def exchange(slot, axis, sends, recvs):
        copies = []
        for way, (step, there) in enumerate(((-1, 1), (1, 0))):
            copy = pltpu.make_async_remote_copy(
                src_ref=sends.at[slot // 2, way],
                dst_ref=recvs.at[slot // 2, there],
                send_sem=halo_send.at[2 * slot + way],
                recv_sem=halo_recv.at[2 * slot + there],
                device_id=side(axis, step),
                device_id_type=MESH,
            )
            copy.start()
            copies.append(copy)
        for copy in copies:
            copy.wait()

    pl.semaphore_wait(barrier, len(greet))

    def put_rows(at, field, first, second):
        hs_row[at, 0] = field[first : first + HALF, 0:pcol, :].reshape(HALF * pcol, channels).astype(BF)
        hs_row[at, 1] = field[second : second + HALF, 0:pcol, :].reshape(HALF * pcol, channels).astype(BF)

    def put_cols(at, field):
        hs_col[at, 0] = field[:, 0:WIN, :].reshape(prow * WIN, channels).astype(BF)
        hs_col[at, 1] = field[:, pcol - WIN : pcol, :].reshape(prow * WIN, channels).astype(BF)

    def got_row(at, way):
        return hr_row[at, way].astype(F32).reshape(HALF, pcol, channels)

    def got_col(at, way):
        return hr_col[at, way].astype(F32).reshape(prow, WIN, channels)

    put_rows(0, f1, HALF, rows)
    exchange(0, "row", hs_row, hr_row)
    f1[0:HALF, 0:pcol, :] = got_row(0, 0)
    f1[prow - HALF : prow, 0:pcol, :] = got_row(0, 1)
    put_cols(0, f1)
    exchange(1, "col", hs_col, hr_col)
    upper_half = lax.broadcasted_iota(jnp.int32, (prow, WIN, channels), 1) >= HALF
    f1[:, 0:WIN, :] = jnp.where(upper_half, f1[:, 0:WIN, :], got_col(0, 0))
    f1[:, pcol - WIN : pcol, :] = jnp.where(
        upper_half, got_col(0, 1), f1[:, pcol - WIN : pcol, :]
    )

    for j in range(n1):
        spots = spots1(j)
        scatter(h1, spots, attn_forward(gather(f1, spots), 1, n0 + j, usable1(j)))

    for j in range(rows // strip):
        inner = pl.ds(HALF + j * strip, strip)
        h = h1[inner, HALF : HALF + cols, :].reshape(flat, channels)
        g = cot[pl.ds(j * strip, strip)].astype(F32).reshape(flat, channels)
        result, saved = feed_forward(h, 1)
        dh = feed_backward(saved, g, 1)
        out[pl.ds(j * strip, strip)] = result.reshape(strip, cols, channels).astype(BF)
        dh1[inner, HALF : HALF + cols, :] = dh.reshape(strip, cols, channels)

    for j in range(n1):
        spots = spots1(j)
        scatter(g1, spots, attn_backward(gather(dh1, spots), 1, n0 + j))

    pack_grads(1)
    high = reduce_steps(1)
    next(high, None)
    put_cols(1, g1)
    exchange(3, "col", hs_col, hr_col)
    g1[:, 0:WIN, :] += got_col(1, 0)
    g1[:, pcol - WIN : pcol, :] += got_col(1, 1)
    next(high, None)
    put_rows(1, g1, 0, prow - HALF)
    exchange(2, "row", hs_row, hr_row)
    g1[HALF : 2 * HALF, 0:pcol, :] += got_row(1, 0)
    g1[rows : rows + HALF, 0:pcol, :] += got_row(1, 1)
    next(high, None)

    for j in range(rows // strip):
        here = pl.ds(j * strip, strip)
        g = g1[pl.ds(HALF + j * strip, strip), HALF : HALF + cols, :].reshape(flat, channels)
        dh = feed_backward((fx[j], fr[j], ff[j], fm[j], fs[j]), g, 0)
        h0[here] = dh.reshape(strip, cols, channels)
        if j % 2:
            next(high, None)

    for j in range(n0):
        spots = spots0(j)
        scatter(grad_region, spots, attn_backward(gather(h0, spots), 0, j))
        next(high, None)

    pack_grads(0)
    low = reduce_steps(0)
    next(low, None)
    for _ in high:
        pass
    for _ in low:
        pass

def finish(
    out, grad_region, low, high, o_out, o_region, o_gains, o_qkv, o_qkv_bias, o_table, o_proj, o_up, o_up_bias, o_down
):
    channels = out.shape[2]
    o_out[...] = out[...]
    o_region[...] = grad_region[...]
    hots = [offsets(c) for c in range(WIN)]
    for b, source in enumerate((low, high)):

        def fetch(unit, n, width=128):
            return source[unit : unit + n].astype(F32).reshape(n * 16, 128)[:, :width]

        o_qkv[b] = jnp.concatenate([fetch(U_QKV + 6 * t, 6, channels) for t in range(3)], 1)
        for t in range(3):
            o_up[b, :, t * 128 : (t + 1) * 128] = fetch(U_UP + 6 * t, 6)
            o_down[b, :, t * 128 : (t + 1) * 128] = fetch(U_DOWN + 6 * t, 6)
        o_proj[b] = fetch(U_PROJ, 6, channels)
        small = fetch(U_SMALL, 2)
        o_gains[b] = small[3:5, :channels]
        o_qkv_bias[b : b + 1, :] = jnp.concatenate([small[t : t + 1, :channels] for t in range(3)], 1)
        for t in range(3):
            o_up_bias[b : b + 1, t * 128 : (t + 1) * 128] = small[5 + t : 6 + t]
        tables = small[8:32]
        row = lax.rem(lax.broadcasted_iota(jnp.int32, tables.shape, 0), WIN)
        lane = lax.broadcasted_iota(jnp.int32, tables.shape, 1)
        total = None
        for c in range(WIN):
            mine = jnp.where((row == c) & (lane < (2 * WIN - 1) * WIN), tables, 0.0)
            term = dot_nt(mine.astype(BF), hots[c])
            total = term if total is None else total + term
        for h in range(3):
            o_table[b, h : h + 1, :] = jnp.sum(total[h * WIN : (h + 1) * WIN], 0, keepdims=True)


def body(n_row, n_col, region, cotangent, gains, wqkv, bqkv, table, wproj, wup, bup, wdown):
    rows, cols, channels = region.shape
    hidden = wup.shape[2]
    prow, pcol = rows + WIN, cols + WIN
    devices = n_row * n_col
    units = -(-U_BLOCK // devices) * devices
    phases = factors(n_row, n_col)
    sizes = []
    for phase in phases:
        size = 1
        for f in phase:
            size *= f[2]
        sizes.append(size)
    recv, acc, gath = [], [], []
    now = units
    for size in sizes:
        gath.append(pltpu.VMEM((2, now, 16, 128), BF))
        now //= size
        recv.append(pltpu.VMEM((2, size - 1, now, 16, 128), BF))
        acc.append(pltpu.VMEM((2, now, 16, 128), BF))
    turns = cols // (3 * WIN) + (pcol + WIN) // (2 * WIN)
    steps = 2 * sum(s - 1 for s in sizes)
    vmem = pl.BlockSpec(memory_space=pltpu.VMEM)
    shapes = [
        jax.ShapeDtypeStruct((rows, cols, channels), BF),
        jax.ShapeDtypeStruct((rows, cols, channels), F32),
        jax.ShapeDtypeStruct((units, 16, 128), BF),
        jax.ShapeDtypeStruct((units, 16, 128), BF),
    ]
    field0 = pltpu.VMEM((rows, cols, channels), F32)
    field1 = pltpu.VMEM((prow, pcol + WIN, channels), F32)
    results = pl.pallas_call(
        functools.partial(kernel, n_row, n_col, units),
        out_shape=shapes,
        in_specs=[vmem] * 10,
        out_specs=[vmem] * len(shapes),
        scratch_shapes=[
            pltpu.VMEM((2, 3, channels, channels), BF),
            pltpu.VMEM((2, 3, WIN, 128), F32),
            pltpu.VMEM((2, 3 * TOK, 2 * TOK), F32),
            field0,
            field0,
            field1,
            field1,
            field1,
            field1,
            pltpu.VMEM((2, 3, channels, channels), F32),
            pltpu.VMEM((2, channels, channels), F32),
            pltpu.VMEM((2, channels, hidden), F32),
            pltpu.VMEM((2, channels, hidden), F32),
            pltpu.VMEM((2, 8, channels), F32),
            pltpu.VMEM((2, hidden), F32),
            pltpu.VMEM((2, 3 * TOK, 2 * TOK), F32),
            pltpu.VMEM((2, 2, HALF * pcol, channels), BF),
            pltpu.VMEM((2, 2, HALF * pcol, channels), BF),
            pltpu.VMEM((2, 2, prow * WIN, channels), BF),
            pltpu.VMEM((2, 2, prow * WIN, channels), BF),
            pltpu.SemaphoreType.DMA((8,)),
            pltpu.SemaphoreType.DMA((8,)),
            pltpu.VMEM((2, units, 16, 128), BF),
            *[pltpu.VMEM((turns, GROUP * TOK, channels), BF)] * 3,
            pltpu.VMEM((turns, GROUP // 2, 3 * TOK, 2 * TOK), F32),
            *[pltpu.VMEM((turns, GROUP * TOK, channels), BF)] * 2,
            *[pltpu.VMEM((turns, GROUP * TOK, channels), F32)] * 2,
            *[pltpu.VMEM((rows // 4, 4 * cols, channels), F32)] * 2,
            pltpu.VMEM((rows // 4, 4 * cols, channels), BF),
            pltpu.VMEM((rows // 4, 4 * cols, hidden), BF),
            pltpu.VMEM((rows // 4, 4 * cols, hidden), F32),
            *recv,
            *acc,
            *gath,
            pltpu.SemaphoreType.DMA((2, steps)),
            pltpu.SemaphoreType.DMA((2, steps)),
        ],
        compiler_params=pltpu.CompilerParams(
            collective_id=0, has_side_effects=True, vmem_limit_bytes=48 * 1024 * 1024
        ),
        name="swin_pair",
    )(region, cotangent, gains, wqkv, bqkv, table, wproj, wup, bup, wdown.transpose(0, 2, 1))
    finals = [
        *shapes[:2],
        jax.ShapeDtypeStruct((2, 2, channels), F32),
        jax.ShapeDtypeStruct((2, channels, 3 * channels), F32),
        jax.ShapeDtypeStruct((2, 3 * channels), F32),
        jax.ShapeDtypeStruct(table.shape, F32),
        jax.ShapeDtypeStruct((2, channels, channels), F32),
        jax.ShapeDtypeStruct((2, channels, hidden), F32),
        jax.ShapeDtypeStruct((2, hidden), F32),
        jax.ShapeDtypeStruct((2, channels, hidden), F32),
    ]
    results = pl.pallas_call(
        finish,
        out_shape=finals,
        in_specs=[vmem] * 4,
        out_specs=[vmem] * len(finals),
        compiler_params=pltpu.CompilerParams(vmem_limit_bytes=32 * 1024 * 1024),
        name="finish",
    )(*results)
    return (*results[:9], results[9].transpose(0, 2, 1))


def solution(mesh):
    tile = P("row", "col", None)
    return jax.shard_map(
        functools.partial(body, mesh.shape["row"], mesh.shape["col"]),
        mesh=mesh,
        in_specs=(tile, tile) + (P(),) * 8,
        out_specs=(tile, tile) + (P(),) * 8,
        check_vma=False,
    )
```

```python
import functools

import jax
import jax.numpy as jnp
from jax import lax
from jax.experimental import pallas as pl
from jax.experimental.pallas import tpu as pltpu
from jax.sharding import PartitionSpec as P

WIN = 8
HALF = 4
TOK = 64
BF = jnp.bfloat16
F32 = jnp.float32
MESH = pl.DeviceIdType.MESH
GROUP = 6

U_QKV = 0
U_PROJ = 18
U_UP = 24
U_DOWN = 42
U_SMALL = 60
U_BLOCK = 62


def dot_nn(a, b):
    return lax.dot_general(a, b, (((1,), (0,)), ((), ())), preferred_element_type=F32)


def dot_nt(a, b):
    return lax.dot_general(a, b, (((1,), (1,)), ((), ())), preferred_element_type=F32)


def dot_tn(a, b):
    return lax.dot_general(a, b, (((0,), (0,)), ((), ())), preferred_element_type=F32)


def norm(x):
    average = jnp.mean(x, -1, keepdims=True)
    centred = x - average
    rstd = lax.rsqrt(jnp.mean(centred * centred, -1, keepdims=True) + 1e-05)
    return centred * rstd, rstd


def norm_back(dy, gain, xhat, rstd):
    dx = dy * gain
    return rstd * (
        dx - jnp.mean(dx, -1, keepdims=True) - xhat * jnp.mean(dx * xhat, -1, keepdims=True)
    )


def per_head(fn, x):
    return [fn(x[h * TOK : (h + 1) * TOK], 0, keepdims=True) for h in range(3)]


def by_head(op, x, parts):
    return jnp.concatenate(
        [op(x[h * TOK : (h + 1) * TOK], parts[h]) for h in range(3)], 0
    )


def softmax(s):
    e = by_head(lambda x, top: jnp.exp(x - top), s, per_head(jnp.max, s))
    return by_head(lambda x, total: x * (1.0 / total), e, per_head(jnp.sum, e))


def head_masks(channels):
    lane = lax.broadcasted_iota(jnp.int32, (1, channels), 1)
    size = channels // 3
    return [((lane >= h * size) & (lane < (h + 1) * size)) for h in range(3)]


def stack_heads(x, masks):
    zero = jnp.zeros_like(x)
    return jnp.concatenate([jnp.where(m, x, zero) for m in masks], 0)


def fold_heads(x, masks):
    out = jnp.where(masks[0], x[:TOK], 0.0)
    for h in (1, 2):
        out = out + jnp.where(masks[h], x[h * TOK : (h + 1) * TOK], 0.0)
    return out


def offsets(c):
    side = 2 * WIN - 1
    shape = (side * side, 128)
    lane = lax.broadcasted_iota(jnp.int32, shape, 1)
    entry = lax.broadcasted_iota(jnp.int32, shape, 0)
    wanted = lax.div(lane, WIN) * side + lax.rem(lane, WIN) + (WIN - 1 - c)
    return jnp.where((entry == wanted) & (lane < side * WIN), 1.0, 0.0).astype(BF)


def factors(n_row, n_col):
    phases = [[("col", 1, 2)], [("col", 2, 2), ("row", 1, n_row)], [("col", 4, n_col // 4)]]
    phases = [[f for f in p if f[2] > 1] for p in phases]
    return [p for p in phases if p]


def kernel(
    n_row,
    n_col,
    units,
    region,
    cot,
    gains,
    wqkv,
    bqkv,
    table,
    wproj,
    wup,
    bup,
    wdown,
    out,
    grad_region,
    o_low,
    o_high,
    ws,
    xtab,
    bias,
    f0,
    h0,
    f1,
    h1,
    dh1,
    g1,
    a_qkv,
    a_proj,
    a_up,
    a_down,
    a_vec,
    a_bup,
    a_bias,
    hs_row,
    hr_row,
    hs_col,
    hr_col,
    halo_send,
    halo_recv,
    pack,
    sq,
    sk,
    sv,
    sp,
    smix,
    sa,
    sx,
    sr,
    fx,
    fr,
    ff,
    fm,
    fs,
    *rest,
):
    rows, cols, channels = region.shape
    prow, pcol = rows + WIN, cols + WIN
    wide = pcol + WIN
    scale = (channels // 3) ** (-0.5)
    phases = factors(n_row, n_col)
    n_ph = len(phases)
    rs_recv = rest[:n_ph]
    rs_acc = rest[n_ph : 2 * n_ph]
    ag_buf = rest[2 * n_ph : 3 * n_ph]
    red_send, red_recv = rest[3 * n_ph :]
    index = {"row": lax.axis_index("row"), "col": lax.axis_index("col")}
    count = {"row": n_row, "col": n_col}

    def device(changes):
        where = dict(index)
        where.update(changes)
        return (where["row"], where["col"])

    def side(axis, step):
        n = count[axis]
        return device({axis: lax.rem(index[axis] + (step + n), n)})

    def members(phase):
        size = 1
        me = 0
        for _, stride, n in phase:
            size *= n
        partners = []
        digits = []
        for axis, stride, n in phase:
            digit = lax.rem(lax.div(index[axis], stride), n)
            digits.append(digit)
            me = me * n + digit
        for d in range(1, size):
            rest_d, ds = d, []
            for _, _, n in reversed(phase):
                ds.append(rest_d % n)
                rest_d //= n
            ds = ds[::-1]
            neg = 0
            member = 0
            changes = {}
            for (axis, stride, n), digit, step in zip(phase, digits, ds):
                neg = neg * n + (-step) % n
                other = lax.rem(digit + step, n)
                member = member * n + other
                changes[axis] = changes.get(axis, index[axis]) + (other - digit) * stride
            partners.append((d, neg, member, device(changes)))
        return size, me, partners

    groups = [members(p) for p in phases]

    barrier = pltpu.get_barrier_semaphore()
    greet = [side("col", -1), side("col", 1), side("row", -1), side("row", 1)]
    for _, _, partners in groups:
        greet += [p[3] for p in partners]
    for dev in greet:
        pl.semaphore_signal(barrier, inc=1, device_id=dev, device_id_type=MESH)

    for ref in (a_qkv, a_proj, a_up, a_down, a_vec, a_bup, a_bias, dh1, f1, pack):
        ref[...] = jnp.zeros(ref.shape, ref.dtype)
    terms = []
    left_over = table[...].reshape(6, table.shape[2])
    for _ in range(3):
        terms.append(left_over.astype(BF))
        left_over = left_over - terms[-1].astype(F32)
    for c in range(WIN):
        hot = offsets(c)
        line = dot_nn(terms[0], hot) + dot_nn(terms[1], hot) + dot_nn(terms[2], hot)
        for n in range(6):
            xtab[n // 3, n % 3, c : c + 1, :] = line[n : n + 1]
    for b in range(2):
        whole = wqkv[b].astype(F32)
        for t in range(3):
            ws[b, t] = whole[:, t * channels : (t + 1) * channels].astype(BF)
        for r in range(WIN):
            at = (WIN - 1 - r) * WIN
            for h in range(3):
                part = xtab[b, h][:, at : at + TOK]
                bias[b, h * TOK + r * WIN : h * TOK + (r + 1) * WIN, :] = jnp.concatenate(
                    [part, part], 1
                )
    f0[...] = region[...].astype(F32)
    masks = head_masks(channels)

    def qkv_of(u, b):
        xhat, rstd = norm(u)
        a = (xhat * gains[b, 0:1, :]).astype(BF)
        line = bqkv[b : b + 1, :]
        parts = [
            (dot_nn(a, ws[b, t]) + line[:, t * channels : (t + 1) * channels]).astype(BF)
            for t in range(3)
        ]
        return xhat, rstd, a, parts

    def split(x, w):
        return x[w * TOK : (w + 1) * TOK]

    left = lax.broadcasted_iota(jnp.int32, (3 * TOK, 2 * TOK), 1) < TOK

    def pair_product(first, second, both):
        return jnp.where(left, dot_nt(first, both), dot_nt(second, both))

    def pair_rows(x, first, second):
        return jnp.concatenate([dot_tn(x, first)[:TOK], dot_tn(x, second)[TOK:]], 0)

    def pair_sum(x, both):
        rest_rows = jnp.zeros_like(both[:TOK])
        one = dot_nn(x, jnp.concatenate([both[:TOK], rest_rows], 0))
        two = dot_nn(x, jnp.concatenate([rest_rows, both[TOK:]], 0))
        return [fold_heads(one, masks), fold_heads(two, masks)]

    def stacked(x, w):
        return stack_heads(split(x, w), masks), stack_heads(split(x, w + 1), masks)

    def attn_forward(u, b, at, usable):
        xhat, rstd, a, (q, k, v) = qkv_of(u, b)
        sq[at], sk[at], sv[at], sa[at] = q, k, v, a
        sx[at] = xhat
        sr[at] = jnp.broadcast_to(rstd, xhat.shape)
        mixed = []
        for w in range(0, GROUP, 2):
            both = q[w * TOK : (w + 2) * TOK]
            s = pair_product(*stacked(k, w), both) * scale + bias[b]
            if usable is not None:
                s = jnp.where(usable(w), s, -1e30)
            p = softmax(s)
            sp[at, w // 2] = p
            mixed.append(pair_rows(p.astype(BF), *stacked(v, w)))
        mixed = jnp.concatenate(mixed, 0).astype(BF)
        smix[at] = mixed
        return u + dot_nn(mixed, wproj[b])

    def attn_backward(dh, b, at):
        xhat, rstd, a, q, k, v = sx[at], sr[at], sa[at], sq[at], sk[at], sv[at]
        dhb = dh.astype(BF)
        dmix = dot_nt(dhb, wproj[b]).astype(BF)
        a_proj[b] += dot_tn(smix[at], dhb)
        dqs, dks, dvs = [], [], []
        dbias = None
        for w in range(0, GROUP, 2):
            both, do = q[w * TOK : (w + 2) * TOK], dmix[w * TOK : (w + 2) * TOK]
            p = sp[at, w // 2]
            dp = pair_product(*stacked(v, w), do)
            ds = p * by_head(jnp.subtract, dp, per_head(jnp.sum, dp * p))
            dbias = ds if dbias is None else dbias + ds
            dsb = (ds * scale).astype(BF)
            dqs.append(pair_rows(dsb, *stacked(k, w)))
            dks += pair_sum(dsb, both)
            dvs += pair_sum(p.astype(BF), do)
        a_bias[b] += dbias
        da = None
        for t, parts in enumerate((dqs, dks, dvs)):
            grad = jnp.concatenate(parts, 0)
            a_vec[b, t : t + 1, :] += jnp.sum(grad, 0, keepdims=True)
            grad = grad.astype(BF)
            a_qkv[b, t] += dot_tn(a, grad)
            term = dot_nt(grad, ws[b, t])
            da = term if da is None else da + term
        a_vec[b, 3:4, :] += jnp.sum(da * xhat, 0, keepdims=True)
        return dh + norm_back(da, gains[b, 0:1, :], xhat, rstd)

    def gelu(z):
        t = jnp.tanh(0.7978845608028654 * z * (1.0 + 0.044715 * z * z))
        return t, 0.5 * z * (1.0 + t)

    def slope_of(z, t):
        return 0.5 * (1.0 + t) + 0.5 * z * (1.0 - t * t) * (
            0.7978845608028654 * (1.0 + 0.134145 * z * z)
        )

    def feed_forward(h, b):
        xhat, rstd = norm(h)
        f = (xhat * gains[b, 1:2, :]).astype(BF)
        z = dot_nn(f, wup[b]) + bup[b : b + 1, :]
        t, m = gelu(z)
        m = m.astype(BF)
        return h + dot_nt(m, wdown[b]), (xhat, rstd, f, m, slope_of(z, t))

    def feed_backward(saved, g, b):
        xhat, rstd, f, m, slope = saved
        gb = g.astype(BF)
        dz = dot_nn(gb, wdown[b]) * slope
        a_bup[b : b + 1, :] += jnp.sum(dz, 0, keepdims=True)
        dz = dz.astype(BF)
        a_down[b] += dot_tn(gb, m)
        a_up[b] += dot_tn(f, dz)
        df = dot_nt(dz, wup[b])
        a_vec[b, 4:5, :] += jnp.sum(df * xhat, 0, keepdims=True)
        return g + norm_back(df, gains[b, 1:2, :], xhat, rstd)

    def spots0(j):
        return [
            (i * WIN, pl.multiple_of((j * 3 + c) * WIN, WIN))
            for i in range(rows // WIN)
            for c in range(3)
        ]

    def spots1(j):
        return [
            (i * WIN, pl.multiple_of((j * 2 + c) * WIN, WIN))
            for i in range(prow // WIN)
            for c in range(2)
        ]

    def gather(ref, spots):
        return jnp.concatenate(
            [ref[r : r + WIN, pl.ds(c, WIN), :].reshape(TOK, channels) for r, c in spots], 0
        )

    def scatter(ref, spots, x):
        for w, (r, c) in enumerate(spots):
            ref[r : r + WIN, pl.ds(c, WIN), :] = split(x, w).reshape(WIN, WIN, channels)

    key = lax.broadcasted_iota(jnp.int32, (3 * TOK, 2 * TOK), 0)
    key_row = lax.div(lax.rem(key, TOK), WIN) + (index["row"] * rows - HALF)
    key_col = lax.rem(key, WIN) + jnp.where(left, 0, WIN) + (index["col"] * cols - HALF)

    def usable1(j):
        def usable(w):
            row = key_row + (w // 2) * WIN
            col = key_col + j * (2 * WIN)
            return (row >= 0) & (row < n_row * rows) & (col >= 0) & (col < n_col * cols)

        return usable

    n0 = cols // (3 * WIN)
    n1 = wide // (2 * WIN)
    strip = 4
    flat = strip * cols

    def stow(b, unit, x, width):
        n = x.shape[0] // 16
        for t in range((width + 127) // 128):
            part = x[:, t * 128 : min(width, (t + 1) * 128)]
            wide = part.shape[1]
            pack[b, unit + t * n : unit + (t + 1) * n, :, 0:wide] = part.reshape(n, 16, wide).astype(BF)

    hidden = wup.shape[2]
    def pack_grads(b):
        for t in range(3):
            stow(b, U_QKV + 6 * t, a_qkv[b, t], channels)
        stow(b, U_PROJ, a_proj[b], channels)
        stow(b, U_UP, a_up[b], hidden)
        stow(b, U_DOWN, a_down[b], hidden)
        heads = []
        for h in range(3):
            total = None
            for r in range(WIN):
                at = (WIN - 1 - r) * WIN
                line = h * TOK + r * WIN
                part = a_bias[b, line : line + WIN, :]
                part = part[:, :TOK] + part[:, TOK:]
                pieces = [part, jnp.zeros((WIN, 128 - at - TOK), F32)]
                if at:
                    pieces = [jnp.zeros((WIN, at), F32)] + pieces
                part = jnp.concatenate(pieces, 1)
                total = part if total is None else total + part
            heads.append(total)
        vec = jnp.concatenate([a_vec[b], jnp.zeros((WIN, 128 - channels), F32)], 1)
        sub = lax.broadcasted_iota(jnp.int32, (WIN, 128), 0)
        for t in range(3):
            vec = jnp.where(sub == 5 + t, a_bup[b : b + 1, t * 128 : (t + 1) * 128], vec)
        small = jnp.concatenate([vec] + heads, 0)
        stow(b, U_SMALL, small, 128)

    def reduce_steps(b):
        source = pack.at[b]
        size_now = units
        at_sem = 0
        for ph, (size, me, partners) in enumerate(groups):
            part = size_now // size
            copies = []
            for d, neg, member, dev in partners:
                copy = pltpu.make_async_remote_copy(
                    src_ref=source.at[pl.ds(member * part, part)],
                    dst_ref=rs_recv[ph].at[b, neg - 1],
                    send_sem=red_send.at[b, at_sem + d - 1],
                    recv_sem=red_recv.at[b, at_sem + neg - 1],
                    device_id=dev,
                    device_id_type=MESH,
                )
                copy.start()
                copies.append(copy)
            yield
            total = source[pl.ds(me * part, part)].astype(F32)
            for copy in copies:
                copy.wait()
            for d in range(size - 1):
                total = total + rs_recv[ph][b, d].astype(F32)
            rs_acc[ph][b] = total.astype(BF)
            source = rs_acc[ph].at[b]
            size_now = part
            at_sem += size - 1
        for ph in reversed(range(n_ph)):
            size, me, partners = groups[ph]
            part = size_now
            copies = []
            for d, neg, member, dev in partners:
                copy = pltpu.make_async_remote_copy(
                    src_ref=source,
                    dst_ref=ag_buf[ph].at[b, pl.ds(me * part, part)],
                    send_sem=red_send.at[b, at_sem + d - 1],
                    recv_sem=red_recv.at[b, at_sem + neg - 1],
                    device_id=dev,
                    device_id_type=MESH,
                )
                copy.start()
                copies.append(copy)
            ag_buf[ph][b, pl.ds(me * part, part)] = source[...]
            yield
            for copy in copies:
                copy.wait()
            source = ag_buf[ph].at[b]
            size_now = part * size
            at_sem += size - 1
        (o_low, o_high)[b][...] = source[...]

    @pl.loop(0, n0)
    def _(j):
        spots = spots0(j)
        scatter(h0, spots, attn_forward(gather(f0, spots), 0, j, None))

    @pl.loop(0, rows // strip)
    def _(j):
        h = h0[pl.ds(j * strip, strip)].reshape(flat, channels)
        low, (xhat, rstd, f, m, slope) = feed_forward(h, 0)
        fx[j], ff[j], fm[j], fs[j] = xhat, f, m, slope
        fr[j] = jnp.broadcast_to(rstd, xhat.shape)
        low = low.astype(BF).astype(F32)
        f1[pl.ds(HALF + j * strip, strip), HALF : HALF + cols, :] = low.reshape(
            strip, cols, channels
        )

    def exchange(slot, axis, sends, recvs):
        copies = []
        for way, (step, there) in enumerate(((-1, 1), (1, 0))):
            copy = pltpu.make_async_remote_copy(
                src_ref=sends.at[slot // 2, way],
                dst_ref=recvs.at[slot // 2, there],
                send_sem=halo_send.at[2 * slot + way],
                recv_sem=halo_recv.at[2 * slot + there],
                device_id=side(axis, step),
                device_id_type=MESH,
            )
            copy.start()
            copies.append(copy)
        for copy in copies:
            copy.wait()

    pl.semaphore_wait(barrier, len(greet))

    def put_rows(at, field, first, second):
        hs_row[at, 0] = field[first : first + HALF, 0:pcol, :].reshape(HALF * pcol, channels).astype(BF)
        hs_row[at, 1] = field[second : second + HALF, 0:pcol, :].reshape(HALF * pcol, channels).astype(BF)

    def put_cols(at, field):
        hs_col[at, 0] = field[:, 0:WIN, :].reshape(prow * WIN, channels).astype(BF)
        hs_col[at, 1] = field[:, pcol - WIN : pcol, :].reshape(prow * WIN, channels).astype(BF)

    def got_row(at, way):
        return hr_row[at, way].astype(F32).reshape(HALF, pcol, channels)

    def got_col(at, way):
        return hr_col[at, way].astype(F32).reshape(prow, WIN, channels)

    put_rows(0, f1, HALF, rows)
    exchange(0, "row", hs_row, hr_row)
    f1[0:HALF, 0:pcol, :] = got_row(0, 0)
    f1[prow - HALF : prow, 0:pcol, :] = got_row(0, 1)
    put_cols(0, f1)
    exchange(1, "col", hs_col, hr_col)
    upper_half = lax.broadcasted_iota(jnp.int32, (prow, WIN, channels), 1) >= HALF
    f1[:, 0:WIN, :] = jnp.where(upper_half, f1[:, 0:WIN, :], got_col(0, 0))
    f1[:, pcol - WIN : pcol, :] = jnp.where(
        upper_half, got_col(0, 1), f1[:, pcol - WIN : pcol, :]
    )

    @pl.loop(0, n1)
    def _(j):
        spots = spots1(j)
        scatter(h1, spots, attn_forward(gather(f1, spots), 1, n0 + j, usable1(j)))

    @pl.loop(0, rows // strip)
    def _(j):
        inner = pl.ds(HALF + j * strip, strip)
        h = h1[inner, HALF : HALF + cols, :].reshape(flat, channels)
        g = cot[pl.ds(j * strip, strip)].astype(F32).reshape(flat, channels)
        result, saved = feed_forward(h, 1)
        dh = feed_backward(saved, g, 1)
        out[pl.ds(j * strip, strip)] = result.reshape(strip, cols, channels).astype(BF)
        dh1[inner, HALF : HALF + cols, :] = dh.reshape(strip, cols, channels)

    @pl.loop(0, n1)
    def _(j):
        spots = spots1(j)
        scatter(g1, spots, attn_backward(gather(dh1, spots), 1, n0 + j))

    pack_grads(1)
    high = reduce_steps(1)
    next(high, None)
    put_cols(1, g1)
    exchange(3, "col", hs_col, hr_col)
    g1[:, 0:WIN, :] += got_col(1, 0)
    g1[:, pcol - WIN : pcol, :] += got_col(1, 1)
    next(high, None)
    put_rows(1, g1, 0, prow - HALF)
    exchange(2, "row", hs_row, hr_row)
    g1[HALF : 2 * HALF, 0:pcol, :] += got_row(1, 0)
    g1[rows : rows + HALF, 0:pcol, :] += got_row(1, 1)
    next(high, None)

    @pl.loop(0, rows // strip)
    def _(j):
        here = pl.ds(j * strip, strip)
        g = g1[pl.ds(HALF + j * strip, strip), HALF : HALF + cols, :].reshape(flat, channels)
        dh = feed_backward((fx[j], fr[j], ff[j], fm[j], fs[j]), g, 0)
        h0[here] = dh.reshape(strip, cols, channels)

    next(high, None)

    @pl.loop(0, n0)
    def _(j):
        spots = spots0(j)
        scatter(grad_region, spots, attn_backward(gather(h0, spots), 0, j))

    next(high, None)

    pack_grads(0)
    low = reduce_steps(0)
    for _ in low:
        next(high, None)
    for _ in high:
        pass

def finish(
    out, grad_region, low, high, o_out, o_region, o_gains, o_qkv, o_qkv_bias, o_table, o_proj, o_up, o_up_bias, o_down
):
    channels = out.shape[2]
    o_out[...] = out[...]
    o_region[...] = grad_region[...]
    hots = [offsets(c) for c in range(WIN)]
    for b, source in enumerate((low, high)):

        def fetch(unit, n, width=128):
            return source[unit : unit + n].astype(F32).reshape(n * 16, 128)[:, :width]

        o_qkv[b] = jnp.concatenate([fetch(U_QKV + 6 * t, 6, channels) for t in range(3)], 1)
        for t in range(3):
            o_up[b, :, t * 128 : (t + 1) * 128] = fetch(U_UP + 6 * t, 6)
            o_down[b, :, t * 128 : (t + 1) * 128] = fetch(U_DOWN + 6 * t, 6)
        o_proj[b] = fetch(U_PROJ, 6, channels)
        small = fetch(U_SMALL, 2)
        o_gains[b] = small[3:5, :channels]
        o_qkv_bias[b : b + 1, :] = jnp.concatenate([small[t : t + 1, :channels] for t in range(3)], 1)
        for t in range(3):
            o_up_bias[b : b + 1, t * 128 : (t + 1) * 128] = small[5 + t : 6 + t]
        tables = small[8:32]
        row = lax.rem(lax.broadcasted_iota(jnp.int32, tables.shape, 0), WIN)
        lane = lax.broadcasted_iota(jnp.int32, tables.shape, 1)
        total = None
        for c in range(WIN):
            mine = jnp.where((row == c) & (lane < (2 * WIN - 1) * WIN), tables, 0.0)
            term = dot_nt(mine.astype(BF), hots[c])
            total = term if total is None else total + term
        for h in range(3):
            o_table[b, h : h + 1, :] = jnp.sum(total[h * WIN : (h + 1) * WIN], 0, keepdims=True)


def body(n_row, n_col, region, cotangent, gains, wqkv, bqkv, table, wproj, wup, bup, wdown):
    rows, cols, channels = region.shape
    hidden = wup.shape[2]
    prow, pcol = rows + WIN, cols + WIN
    devices = n_row * n_col
    units = -(-U_BLOCK // devices) * devices
    phases = factors(n_row, n_col)
    sizes = []
    for phase in phases:
        size = 1
        for f in phase:
            size *= f[2]
        sizes.append(size)
    recv, acc, gath = [], [], []
    now = units
    for size in sizes:
        gath.append(pltpu.VMEM((2, now, 16, 128), BF))
        now //= size
        recv.append(pltpu.VMEM((2, size - 1, now, 16, 128), BF))
        acc.append(pltpu.VMEM((2, now, 16, 128), BF))
    turns = cols // (3 * WIN) + (pcol + WIN) // (2 * WIN)
    steps = 2 * sum(s - 1 for s in sizes)
    vmem = pl.BlockSpec(memory_space=pltpu.VMEM)
    shapes = [
        jax.ShapeDtypeStruct((rows, cols, channels), BF),
        jax.ShapeDtypeStruct((rows, cols, channels), F32),
        jax.ShapeDtypeStruct((units, 16, 128), BF),
        jax.ShapeDtypeStruct((units, 16, 128), BF),
    ]
    field0 = pltpu.VMEM((rows, cols, channels), F32)
    field1 = pltpu.VMEM((prow, pcol + WIN, channels), F32)
    results = pl.pallas_call(
        functools.partial(kernel, n_row, n_col, units),
        out_shape=shapes,
        in_specs=[vmem] * 10,
        out_specs=[vmem] * len(shapes),
        scratch_shapes=[
            pltpu.VMEM((2, 3, channels, channels), BF),
            pltpu.VMEM((2, 3, WIN, 128), F32),
            pltpu.VMEM((2, 3 * TOK, 2 * TOK), F32),
            field0,
            field0,
            field1,
            field1,
            field1,
            field1,
            pltpu.VMEM((2, 3, channels, channels), F32),
            pltpu.VMEM((2, channels, channels), F32),
            pltpu.VMEM((2, channels, hidden), F32),
            pltpu.VMEM((2, channels, hidden), F32),
            pltpu.VMEM((2, 8, channels), F32),
            pltpu.VMEM((2, hidden), F32),
            pltpu.VMEM((2, 3 * TOK, 2 * TOK), F32),
            pltpu.VMEM((2, 2, HALF * pcol, channels), BF),
            pltpu.VMEM((2, 2, HALF * pcol, channels), BF),
            pltpu.VMEM((2, 2, prow * WIN, channels), BF),
            pltpu.VMEM((2, 2, prow * WIN, channels), BF),
            pltpu.SemaphoreType.DMA((8,)),
            pltpu.SemaphoreType.DMA((8,)),
            pltpu.VMEM((2, units, 16, 128), BF),
            *[pltpu.VMEM((turns, GROUP * TOK, channels), BF)] * 3,
            pltpu.VMEM((turns, GROUP // 2, 3 * TOK, 2 * TOK), F32),
            *[pltpu.VMEM((turns, GROUP * TOK, channels), BF)] * 2,
            *[pltpu.VMEM((turns, GROUP * TOK, channels), F32)] * 2,
            *[pltpu.VMEM((rows // 4, 4 * cols, channels), F32)] * 2,
            pltpu.VMEM((rows // 4, 4 * cols, channels), BF),
            pltpu.VMEM((rows // 4, 4 * cols, hidden), BF),
            pltpu.VMEM((rows // 4, 4 * cols, hidden), F32),
            *recv,
            *acc,
            *gath,
            pltpu.SemaphoreType.DMA((2, steps)),
            pltpu.SemaphoreType.DMA((2, steps)),
        ],
        compiler_params=pltpu.CompilerParams(
            collective_id=0, has_side_effects=True, vmem_limit_bytes=60 * 1024 * 1024
        ),
        name="swin_pair",
    )(region, cotangent, gains, wqkv, bqkv, table, wproj, wup, bup, wdown.transpose(0, 2, 1))
    finals = [
        *shapes[:2],
        jax.ShapeDtypeStruct((2, 2, channels), F32),
        jax.ShapeDtypeStruct((2, channels, 3 * channels), F32),
        jax.ShapeDtypeStruct((2, 3 * channels), F32),
        jax.ShapeDtypeStruct(table.shape, F32),
        jax.ShapeDtypeStruct((2, channels, channels), F32),
        jax.ShapeDtypeStruct((2, channels, hidden), F32),
        jax.ShapeDtypeStruct((2, hidden), F32),
        jax.ShapeDtypeStruct((2, channels, hidden), F32),
    ]
    results = pl.pallas_call(
        finish,
        out_shape=finals,
        in_specs=[vmem] * 4,
        out_specs=[vmem] * len(finals),
        compiler_params=pltpu.CompilerParams(vmem_limit_bytes=32 * 1024 * 1024),
        name="finish",
    )(*results)
    return (*results[:9], results[9].transpose(0, 2, 1))


def solution(mesh):
    tile = P("row", "col", None)
    return jax.shard_map(
        functools.partial(body, mesh.shape["row"], mesh.shape["col"]),
        mesh=mesh,
        in_specs=(tile, tile) + (P(),) * 8,
        out_specs=(tile, tile) + (P(),) * 8,
        check_vma=False,
    )
```
